256 devices in a mesh: rep: 32 (over x, y, core), tp: 8 (over z).
Axes of the slice: x: 4, y: 4, z: 8, core: 2. Of those that a mesh axis runs over, the one named last changes fastest.
Arguments:
- cache_keys: bfloat16 [1024, 8, 256, 128], P('rep', 'tp'), may hold values from -3 to 3
- cache_values: bfloat16 [1024, 8, 256, 128], P('rep', 'tp'), may hold values from -6 to 6
- cache_lengths: int32 [1024], P('rep'), may hold values from 2 to 256, as said below
- dest_replica: int32 [1024], P('rep'), may hold values from 0 to 31, as said below
- dest_slot: int32 [1024], P('rep'), may hold values from 0 to 31
- queries: bfloat16 [1024, 4, 8192], P('rep', None, 'tp'), may hold values from -7 to 7
- new_keys: bfloat16 [1024, 4, 1024], P('rep', None, 'tp'), may hold values from -6 to 6
- new_values: bfloat16 [1024, 4, 1024], P('rep', None, 'tp'), may hold values from -12 to 12
- out_weight: bfloat16 [8192, 4096], P('tp'), may hold values from -0.75 to 0.75
Outputs:
- layer_out: bfloat16 [1024, 4, 4096], P('rep', None, 'tp')
The draws below stay inside these ranges and needn't reach their ends.
Inputs may be any that keep to these rules, and one draw needn't show every extreme that they name: `cache_lengths`: every row has at least two cached tokens; some row has exactly 256. Row r moves to slot dest_slot[r] of replica dest_replica[r]; together they give a permutation of all places. Each replica receives exactly 32 rows and sends to each replica either none or exactly 2 of its rows.
All inputs are finite; a program needn't handle non-finite values.
Results may differ from the reference program's by a relative error of at most 0.02.
Values may be sent and summed in bfloat16 or wider, within the bound.
No kernel may reach another device: no remote copies, remote signals or barrier semaphores. Data moves between devices by JAX's collectives and lax.ppermute only.
A program may use at most 128 MiB of HBM per device.

```python
import math
import jax
import jax.numpy as jnp
from jax import lax

HEADS = 64
KV_HEADS = 8
HD = 128
DWIN = 4096
SLOTS = 32
CTX = 256
STEPS = 4
ROWS = 1024
CAP = 2
N_REP = 32
N_TP = 8


def route_table(key):
    key = jax.random.fold_in(key, 11)
    keys_all = jax.random.split(key, 5)
    group_total = SLOTS // CAP
    offsets = jax.random.permutation(keys_all[0], N_REP)[:group_total].astype(jnp.int32)
    inner_perm = jax.random.permutation(keys_all[1], N_REP).astype(jnp.int32)
    outer_perm = jax.random.permutation(keys_all[2], N_REP).astype(jnp.int32)
    targets = outer_perm[(inner_perm[:, None] + offsets[None, :]) % N_REP]
    source_perm = jax.vmap(lambda subkey: jax.random.permutation(subkey, SLOTS))(jax.random.split(keys_all[3], N_REP)).astype(jnp.int32)
    landing_perm = jax.vmap(lambda subkey: jax.random.permutation(subkey, SLOTS))(jax.random.split(keys_all[4], N_REP)).astype(jnp.int32)
    places = jnp.arange(SLOTS, dtype=jnp.int32)
    sent_to = targets[:, places // CAP]
    slot_at = landing_perm[sent_to, places[None, :]]
    replicas = jnp.arange(N_REP, dtype=jnp.int32)[:, None]
    dest_rep = jnp.zeros((N_REP, SLOTS), jnp.int32).at[replicas, source_perm].set(sent_to)
    dest_place = jnp.zeros((N_REP, SLOTS), jnp.int32).at[replicas, source_perm].set(slot_at)
    return (dest_rep.reshape(ROWS), dest_place.reshape(ROWS))


def draw_dest_replica(key, part):
    dest_rep, dest_place = route_table(key)
    return dest_rep


def draw_dest_slot(key, part):
    dest_rep, dest_place = route_table(key)
    return dest_place


def draw_cache_lengths(key, part):
    key = jax.random.fold_in(key, 23)
    first_key, second_key = jax.random.split(key)
    drawn = jax.random.randint(first_key, (ROWS,), 2, CTX + 1)
    longest = jax.random.randint(second_key, (), 0, ROWS)
    return jnp.where(jnp.arange(ROWS) == longest, CTX, drawn).astype(jnp.int32)


def draw_cache_keys(key, part):
    key = jax.random.fold_in(key, 31)
    drawn = jnp.clip(jax.random.normal(key, (ROWS, KV_HEADS, CTX, HD), jnp.float32), -3.0, 3.0)
    return drawn.astype(jnp.bfloat16)


def draw_queries(key, part):
    key = jax.random.fold_in(key, 37)
    drawn = jnp.clip(jax.random.normal(key, (ROWS, STEPS, HEADS * HD), jnp.float32), -4.0, 4.0)
    return drawn.astype(jnp.bfloat16)


def strengthened(values, key, source, target, shards_of, factor):
    owner, partner = [(jnp.arange(values.shape[axis_at]) // (values.shape[axis_at] // shards_of)).reshape([-1 if axis == axis_at else 1 for axis in range(values.ndim)]) for axis_at in (source, target)]
    chosen = jax.random.permutation(key, shards_of)[partner]
    strong = (owner == chosen) | (owner == (partner + shards_of // 2) % shards_of)
    return jnp.where(strong, factor * values, values)


def shard_levels(own_key, extent, cuts, low, largest):
    loudness, own = 1.0, jax.random.fold_in(own_key, 6)
    for axis_at, blocks in cuts:
        draws = jnp.exp(jax.random.uniform(jax.random.fold_in(own, axis_at), (blocks,), jnp.float32, low / len(cuts), largest / len(cuts)))
        loudness = loudness * jnp.repeat(draws, extent[axis_at] // blocks).reshape([-1 if axis == axis_at else 1 for axis in range(len(extent))])
    return loudness


def centred(key, shape, scale, limit, cuts=(), kind=jnp.bfloat16):
    values = scale * jax.random.normal(key, shape, jnp.float32)
    if cuts:
        values = values * shard_levels(key, shape, cuts, -0.22, 0.18)
    return jnp.clip(values, -limit, limit).astype(kind)


def bell_draw_with(stream_key, dims, deviation, most, pieces, heavy, kind=jnp.bfloat16):
    values = deviation * jax.random.normal(stream_key, dims, jnp.float32)
    if pieces:
        values = values * shard_levels(stream_key, dims, pieces, -0.22, 0.18)
    return jnp.clip(strengthened(values, jax.random.fold_in(stream_key, 3), *heavy), -most, most).astype(kind)


def setup_inputs(seed: int = 0) -> dict:
    splits = jax.random.split(jax.random.key(seed), 10)
    cache_keys = draw_cache_keys(jax.random.fold_in(splits[9], 71), 0)
    cache_values = centred(splits[1], (ROWS, KV_HEADS, CTX, HD), 1.0, 6.0, ((0, 32), (1, 8)))
    cache_lengths = draw_cache_lengths(jax.random.fold_in(splits[9], 71), 0)
    dest_replica = draw_dest_replica(jax.random.fold_in(splits[9], 71), 0)
    dest_slot = draw_dest_slot(jax.random.fold_in(splits[9], 71), 0)
    queries = draw_queries(jax.random.fold_in(splits[9], 71), 0)
    new_keys = centred(splits[6], (ROWS, STEPS, KV_HEADS * HD), 1.0, 6.0, ((0, 32), (2, 8)))
    new_values = centred(splits[7], (ROWS, STEPS, KV_HEADS * HD), 3.0, 12.0, ((0, 32), (2, 8)))
    out_weight = bell_draw_with(splits[8], (HEADS * HD, DWIN), (HEADS * HD // 64) ** -0.5, 0.75, ((0, 8),), (0, 1, 8, 2.0))
    return {"cache_keys": cache_keys, "cache_values": cache_values, "cache_lengths": cache_lengths, "dest_replica": dest_replica, "dest_slot": dest_slot, "queries": queries, "new_keys": new_keys, "new_values": new_values, "out_weight": out_weight}


MASKED = -1e+30

def cached_part(queries, cache_keys, cache_values, cache_lengths):
    row_count, step_count, feature_count = queries.shape
    kv_heads = cache_keys.shape[1]
    cache_len = cache_keys.shape[2]
    head_size = cache_keys.shape[3]
    group_size = feature_count // (kv_heads * head_size)
    grouped = queries.reshape(row_count, step_count, kv_heads, group_size, head_size).astype(jnp.float32)
    scores = jnp.einsum('stkgd,skcd->stkgc', grouped, cache_keys.astype(jnp.float32)) * (1.0 / math.sqrt(head_size))
    live_keys = jnp.arange(cache_len)[None, :] < cache_lengths[:, None]
    scores = jnp.where(live_keys[:, None, None, None, :], scores, MASKED)
    peak = lax.optimization_barrier(jnp.max(scores, axis=-1))
    weights = jnp.exp(scores - peak[..., None]).astype(jnp.bfloat16)
    weight_sum = lax.optimization_barrier(jnp.sum(weights.astype(jnp.float32), axis=-1))
    summed = jnp.einsum('stkgc,skcd->stkgd', weights.astype(jnp.float32), cache_values.astype(jnp.float32))
    return (peak.reshape(row_count, step_count, -1), weight_sum.reshape(row_count, step_count, -1), summed.reshape(row_count, step_count, feature_count))

def fresh_part(queries, new_keys, new_values, head_size):
    row_count, step_count, feature_count = queries.shape
    kv_heads = new_keys.shape[2] // head_size
    group_size = feature_count // (kv_heads * head_size)
    grouped = queries.reshape(row_count, step_count, kv_heads, group_size, head_size).astype(jnp.float32)
    fresh_keys = new_keys.reshape(row_count, step_count, kv_heads, head_size).astype(jnp.float32)
    fresh_values = new_values.reshape(row_count, step_count, kv_heads, head_size).astype(jnp.float32)
    scores = jnp.einsum('stkgd,sukd->stkgu', grouped, fresh_keys) * (1.0 / math.sqrt(head_size))
    causal = jnp.arange(step_count)[None, :] <= jnp.arange(step_count)[:, None]
    scores = jnp.where(causal[None, :, None, None, :], scores, MASKED)
    peak = lax.optimization_barrier(jnp.max(scores, axis=-1))
    weights = jnp.exp(scores - peak[..., None]).astype(jnp.bfloat16)
    weight_sum = lax.optimization_barrier(jnp.sum(weights.astype(jnp.float32), axis=-1))
    summed = jnp.einsum('stkgu,sukd->stkgd', weights.astype(jnp.float32), fresh_values)
    return (peak.reshape(row_count, step_count, -1), weight_sum.reshape(row_count, step_count, -1), summed.reshape(row_count, step_count, feature_count))

def combine_parts(cache_side, fresh_side, head_size):
    peak = jnp.maximum(cache_side[0], fresh_side[0])
    cache_factor = jnp.exp(cache_side[0] - peak)
    fresh_factor = jnp.exp(fresh_side[0] - peak)
    row_count, step_count, head_count = peak.shape
    numerator = cache_side[2].reshape(row_count, step_count, head_count, head_size) * cache_factor[..., None] + fresh_side[2].reshape(row_count, step_count, head_count, head_size) * fresh_factor[..., None]
    denominator = cache_side[1] * cache_factor + fresh_side[1] * fresh_factor
    attended = numerator / denominator[..., None]
    return attended.reshape(row_count, step_count, head_count * head_size).astype(jnp.bfloat16)

def reference(cache_keys, cache_values, cache_lengths, dest_replica, dest_slot, queries, new_keys, new_values, out_weight):
    landing = (dest_replica * SLOTS + dest_slot).astype(jnp.int32)
    anchor = jnp.zeros((ROWS,), jnp.int32).at[landing].set(jnp.arange(ROWS, dtype=jnp.int32))

    def one_block(block_index):
        start = (block_index * SLOTS).astype(jnp.int32)
        picked = lax.dynamic_slice_in_dim(anchor, start, SLOTS)
        block_queries = lax.dynamic_slice_in_dim(queries, start, SLOTS)
        block_keys = lax.dynamic_slice_in_dim(new_keys, start, SLOTS)
        block_values = lax.dynamic_slice_in_dim(new_values, start, SLOTS)
        cache_side = cached_part(block_queries, jnp.take(cache_keys, picked, axis=0), jnp.take(cache_values, picked, axis=0), jnp.take(cache_lengths, picked))
        fresh_side = fresh_part(block_queries, block_keys, block_values, HD)
        return combine_parts(cache_side, fresh_side, HD)
    attended = lax.map(one_block, jnp.arange(N_REP, dtype=jnp.int32)).reshape(ROWS * STEPS, HEADS * HD)
    share_rows = HEADS * HD // N_TP
    result = jnp.zeros((ROWS * STEPS, DWIN), jnp.float32)
    for group_index in range(N_TP):
        partial_value = jnp.dot(attended[:, group_index * share_rows:(group_index + 1) * share_rows], out_weight[group_index * share_rows:(group_index + 1) * share_rows], preferred_element_type=jnp.float32)
        rounded = lax.optimization_barrier(partial_value.astype(jnp.bfloat16))
        result = result + rounded.astype(jnp.float32)
    return result.reshape(ROWS, STEPS, DWIN).astype(jnp.bfloat16)
```

```python
import math

import jax
import jax.numpy as jnp
from jax import lax
from jax.experimental import pallas as pl
from jax.experimental.pallas import tpu as pltpu
from jax.sharding import PartitionSpec as P

MASKED = -1e30
VMEM_BYTES = 48 * 1024 * 1024
PAIR_CHUNK = 4


def vmem_spec():
    return pl.BlockSpec(memory_space=pltpu.VMEM)


def smem_spec():
    return pl.BlockSpec(memory_space=pltpu.SMEM)


def hbm_spec():
    return pl.BlockSpec(memory_space=pl.ANY)


def params():
    return pltpu.CompilerParams(vmem_limit_bytes=VMEM_BYTES)


def spots_matrix(bits, steps):
    replicas, tokens = bits.shape
    shape = (replicas, 2 * steps, tokens)
    spread = jnp.broadcast_to(bits[:, None, :], shape)
    within = lax.broadcasted_iota(jnp.int32, shape, 1)
    token = lax.broadcasted_iota(jnp.int32, shape, 2)
    bit = jnp.where(within < steps, spread & 1, spread >> 1)
    hot = jnp.where((token % steps) == (within % steps), bit, 0)
    return hot.astype(jnp.float32).astype(jnp.bfloat16).reshape(replicas * 2 * steps, tokens)


def route_kernel(steps, target_ref, slot_ref, wire_ref, bits_ref):
    replicas, tokens = wire_ref.shape
    shape = (replicas, tokens)
    replica = lax.broadcasted_iota(jnp.int32, shape, 0)
    token = lax.broadcasted_iota(jnp.int32, shape, 1)
    row = token // steps
    mine = target_ref[...] == replica
    first = jnp.min(jnp.where(mine, row, tokens), axis=1, keepdims=True)
    early = mine & (row == first)
    late = mine & (row != first)
    slots = jnp.broadcast_to(slot_ref[...], shape)
    early_slot = jnp.max(jnp.where(early, slots, -1), axis=1, keepdims=True)
    late_slot = jnp.max(jnp.where(late, slots, -1), axis=1, keepdims=True)
    bits_ref[...] = jnp.where(early, 1, 0) + jnp.where(late, 2, 0)
    wire_ref[...] = jnp.where(row == early_slot, 1, 0) + jnp.where(row == late_slot, 2, 0)


def pack_kernel(steps, bits_ref, rows_ref, out_ref):
    hot = spots_matrix(bits_ref[...], steps)
    out_ref[...] = jnp.dot(hot, rows_ref[...], preferred_element_type=jnp.float32).astype(
        jnp.bfloat16
    )


def take_back(hot, rows):
    return lax.dot_general(
        hot, rows, (((0,), (0,)), ((), ())), preferred_element_type=jnp.float32
    ).astype(jnp.bfloat16)


def attend_kernel(
    steps,
    lengths_ref,
    bits_ref,
    got_ref,
    keys_hbm,
    values_hbm,
    weight_hbm,
    *rest,
):
    groups = weight_hbm.shape[1] // rest[0].shape[1]
    outs = rest[:groups]
    here, keys, values, weight, attended, key_sem, value_sem, weight_sem = rest[groups:]
    rows, context, head_size = keys.shape
    features = attended.shape[1]
    heads = features // head_size
    width = outs[0].shape[1]
    tokens = rows * steps
    me = lax.axis_index("tp")

    chunks = key_sem.shape[0]
    per = rows // chunks
    key_copies, value_copies, weight_copies = [], [], []
    for c in range(chunks):
        part = pl.ds(c * per, per)
        key_copies.append(pltpu.make_async_copy(keys_hbm.at[part], keys.at[part], key_sem.at[c]))
        value_copies.append(
            pltpu.make_async_copy(values_hbm.at[part], values.at[part], value_sem.at[c])
        )
        key_copies[-1].start()
        value_copies[-1].start()
    for k in range(groups):
        start = pl.multiple_of(lax.rem(me + k, groups) * width, width)
        weight_copies.append(
            pltpu.make_async_copy(
                weight_hbm.at[:, pl.ds(start, width)], weight.at[k], weight_sem.at[k]
            )
        )
        weight_copies[-1].start()

    here[...] = take_back(spots_matrix(bits_ref[...], steps), got_ref[...])

    pair = 2 * steps
    lines = heads * pair
    scale = 1.0 / math.sqrt(head_size) * math.log2(math.e)
    line = lax.broadcasted_iota(jnp.int32, (lines, context), 0) % pair
    column = lax.broadcasted_iota(jnp.int32, (lines, context), 1)
    upper = line < steps
    fresh_line = lax.broadcasted_iota(jnp.int32, (lines, pair), 0) % pair
    fresh_column = lax.broadcasted_iota(jnp.int32, (lines, pair), 1)
    fresh_live = (fresh_line // steps == fresh_column // steps) & (fresh_column <= fresh_line)
    out_upper = lax.broadcasted_iota(jnp.int32, (lines, head_size), 0) % pair < steps

    def score(left, right):
        return lax.dot_general(
            left, right, (((1,), (1,)), ((), ())), preferred_element_type=jnp.float32
        )

    for step in range(rows // 2):
        a, b = 2 * step, 2 * step + 1
        if a % per == 0:
            key_copies[a // per].wait()
            value_copies[a // per].wait()
        block = here[a * steps : a * steps + pair, :]
        queries = jnp.concatenate(
            [block[:, h * head_size : (h + 1) * head_size] for h in range(heads)], axis=0
        )
        new_keys = block[:, features : features + head_size]
        new_values = block[:, features + head_size :]
        limit = jnp.where(upper, lengths_ref[a], lengths_ref[b])
        scores = jnp.where(upper, score(queries, keys[a]), score(queries, keys[b]))
        scores = jnp.where(column < limit, scores * scale, MASKED)
        fresh = jnp.where(fresh_live, score(queries, new_keys) * scale, MASKED)
        peak = jnp.maximum(
            jnp.max(scores, axis=1, keepdims=True), jnp.max(fresh, axis=1, keepdims=True)
        )
        weights = jnp.exp2(scores - peak).astype(jnp.bfloat16)
        fresh_weights = jnp.exp2(fresh - peak).astype(jnp.bfloat16)
        total = jnp.sum(weights.astype(jnp.float32), axis=1, keepdims=True) + jnp.sum(
            fresh_weights.astype(jnp.float32), axis=1, keepdims=True
        )
        summed = jnp.where(
            out_upper,
            jnp.dot(weights, values[a], preferred_element_type=jnp.float32),
            jnp.dot(weights, values[b], preferred_element_type=jnp.float32),
        ) + jnp.dot(fresh_weights, new_values, preferred_element_type=jnp.float32)
        result = (summed / total).astype(jnp.bfloat16)
        for h in range(heads):
            attended[a * steps : a * steps + pair, h * head_size : (h + 1) * head_size] = result[
                h * pair : (h + 1) * pair
            ]

    for k in range(groups):
        weight_copies[k].wait()
        outs[k][...] = jnp.dot(
            attended[...], weight[k], preferred_element_type=jnp.float32
        ).astype(jnp.bfloat16)


def merge_kernel(steps, bits_ref, *refs):
    parts, out_ref = refs[:-1], refs[-1]
    total = parts[0][...].astype(jnp.float32)
    for part in parts[1:]:
        total = total + part[...].astype(jnp.float32)
    hot = spots_matrix(bits_ref[...], steps)
    out_ref[...] = jnp.dot(
        hot, total.astype(jnp.bfloat16), preferred_element_type=jnp.float32
    ).astype(jnp.bfloat16)


def unpack_kernel(steps, bits_ref, got_ref, out_ref):
    out_ref[...] = take_back(spots_matrix(bits_ref[...], steps), got_ref[...])


def on_device(
    cache_keys,
    cache_values,
    cache_lengths,
    dest_replica,
    dest_slot,
    queries,
    new_keys,
    new_values,
    out_weight,
):
    replicas = lax.axis_size("rep")
    groups = lax.axis_size("tp")
    rows, _, context, head_size = cache_keys.shape
    steps, features = queries.shape[1:]
    tokens = rows * steps
    width = out_weight.shape[1] // groups
    spots = replicas * 2 * steps
    bf16 = jnp.bfloat16

    def out(shape, dtype=bf16):
        return jax.ShapeDtypeStruct(shape, dtype)

    def kernel(body, out_shape, in_specs, out_specs=None, scratch=(), cost=None):
        return pl.pallas_call(
            lambda *refs: body(steps, *refs),
            out_shape=out_shape,
            in_specs=in_specs,
            out_specs=vmem_spec() if out_specs is None else out_specs,
            scratch_shapes=scratch,
            compiler_params=params(),
            cost_estimate=cost,
        )

    targets = jnp.repeat(dest_replica, steps).reshape(1, tokens)
    slots = jnp.repeat(dest_slot, steps).reshape(1, tokens)
    wire, bits = kernel(
        route_kernel,
        (out((replicas, tokens), jnp.int32), out((replicas, tokens), jnp.int32)),
        [vmem_spec()] * 2,
        (vmem_spec(), vmem_spec()),
    )(targets, slots)
    wire = lax.all_to_all(wire.reshape(replicas, 1, tokens), "rep", 0, 0, tiled=True)
    wire = wire.reshape(replicas, tokens)

    full = features + 2 * head_size
    moving = jnp.concatenate([queries, new_keys, new_values], axis=2).reshape(tokens, full)
    packed = kernel(pack_kernel, out((spots, full)), [vmem_spec()] * 2)(wire, moving)
    got = lax.all_to_all(packed.reshape(replicas, 2 * steps, full), "rep", 0, 0, tiled=True)

    partials = kernel(
        attend_kernel,
        tuple(out((tokens, width)) for _ in range(groups)),
        [smem_spec(), vmem_spec(), vmem_spec(), hbm_spec(), hbm_spec(), hbm_spec()],
        tuple(vmem_spec() for _ in range(groups)),
        [
            pltpu.VMEM((tokens, full), bf16),
            pltpu.VMEM((rows, context, head_size), bf16),
            pltpu.VMEM((rows, context, head_size), bf16),
            pltpu.VMEM((groups, features, width), bf16),
            pltpu.VMEM((tokens, features), bf16),
            pltpu.SemaphoreType.DMA((PAIR_CHUNK,)),
            pltpu.SemaphoreType.DMA((PAIR_CHUNK,)),
            pltpu.SemaphoreType.DMA((groups,)),
        ],
    )(
        cache_lengths,
        bits,
        got.reshape(spots, full),
        cache_keys.reshape(rows, context, head_size),
        cache_values.reshape(rows, context, head_size),
        out_weight,
    )

    order = sorted(range(1, groups), key=lambda k: -min(k, groups - k))
    arrived = [
        lax.ppermute(partials[k], "tp", [(i, (i + k) % groups) for i in range(groups)])
        for k in order
    ]
    back = kernel(merge_kernel, out((spots, width)), [vmem_spec()] * (groups + 1))(
        bits, partials[0], *arrived
    )
    back = lax.all_to_all(back.reshape(replicas, 2 * steps, width), "rep", 0, 0, tiled=True)
    result = kernel(unpack_kernel, out((tokens, width)), [vmem_spec()] * 2)(
        wire, back.reshape(spots, width)
    )
    return result.reshape(rows, steps, width)


def solution(mesh):
    return jax.shard_map(
        on_device,
        mesh=mesh,
        in_specs=(
            P("rep", "tp", None, None),
            P("rep", "tp", None, None),
            P("rep"),
            P("rep"),
            P("rep"),
            P("rep", None, "tp"),
            P("rep", None, "tp"),
            P("rep", None, "tp"),
            P("tp", None),
        ),
        out_specs=P("rep", None, "tp"),
        check_vma=False,
    )
```

```python
import math

import jax
import jax.numpy as jnp
from jax import lax
from jax.experimental import pallas as pl
from jax.experimental.pallas import tpu as pltpu
from jax.sharding import PartitionSpec as P

MASKED = -1e30
FIRST = (4, 3, 5)
SECOND = (2, 6, 1, 7)
LAST = (0,)
VMEM_BYTES = 24 * 1024 * 1024


def vmem_spec():
    return pl.BlockSpec(memory_space=pltpu.VMEM)


def smem_spec():
    return pl.BlockSpec(memory_space=pltpu.SMEM)


def hbm_spec():
    return pl.BlockSpec(memory_space=pltpu.HBM)


def in_hbm(array):
    return pltpu.with_memory_space_constraint(array, pltpu.HBM)


def params():
    return pltpu.CompilerParams(vmem_limit_bytes=VMEM_BYTES)


def spots_matrix(bits, steps):
    replicas, tokens = bits.shape
    shape = (replicas, 2 * steps, tokens)
    spread = jnp.broadcast_to(bits[:, None, :], shape)
    within = lax.broadcasted_iota(jnp.int32, shape, 1)
    token = lax.broadcasted_iota(jnp.int32, shape, 2)
    bit = jnp.where(within < steps, spread & 1, spread >> 1)
    hot = jnp.where((token % steps) == (within % steps), bit, 0)
    return hot.astype(jnp.float32).astype(jnp.bfloat16).reshape(replicas * 2 * steps, tokens)


def route_kernel(steps, target_hbm, slot_hbm, wire_ref, bits_ref, target_ref, slot_ref, sems):
    replicas, tokens = wire_ref.shape
    copies = [
        pltpu.make_async_copy(target_hbm, target_ref, sems.at[0]),
        pltpu.make_async_copy(slot_hbm, slot_ref, sems.at[1]),
    ]
    for copy in copies:
        copy.start()
    rows = tokens // steps
    shape = (replicas, tokens)
    spread = lax.broadcasted_iota(jnp.int32, (rows, tokens), 1) // steps
    spread = spread == lax.broadcasted_iota(jnp.int32, (rows, tokens), 0)
    spread = spread.astype(jnp.float32).astype(jnp.bfloat16)
    for copy in copies:
        copy.wait()
    both = jnp.where(
        lax.broadcasted_iota(jnp.int32, (8, rows), 0) == 0, target_ref[...], slot_ref[...]
    )
    both = jnp.dot(
        both.astype(jnp.float32).astype(jnp.bfloat16), spread, preferred_element_type=jnp.float32
    ).astype(jnp.int32)
    replica = lax.broadcasted_iota(jnp.int32, shape, 0)
    row = lax.broadcasted_iota(jnp.int32, shape, 1) // steps
    mine = both[0:1] == replica
    first = jnp.min(jnp.where(mine, row, tokens), axis=1, keepdims=True)
    early = mine & (row == first)
    late = mine & (row != first)
    slots = jnp.broadcast_to(both[1:2], shape)
    early_slot = jnp.max(jnp.where(early, slots, -1), axis=1, keepdims=True)
    late_slot = jnp.max(jnp.where(late, slots, -1), axis=1, keepdims=True)
    bits_ref[...] = jnp.where(early, 1, 0) + jnp.where(late, 2, 0)
    wire_ref[...] = jnp.where(row == early_slot, 1, 0) + jnp.where(row == late_slot, 2, 0)


def pack_kernel(steps, bits_ref, rows_ref, out_ref):
    hot = spots_matrix(bits_ref[...], steps)
    out_ref[...] = jnp.dot(hot, rows_ref[...], preferred_element_type=jnp.float32).astype(
        jnp.bfloat16
    )


def take_back(hot, rows):
    return lax.dot_general(
        hot, rows, (((0,), (0,)), ((), ())), preferred_element_type=jnp.float32
    ).astype(jnp.bfloat16)


def column_copies(offsets, weight_hbm, weight, sems):
    me = lax.axis_index("tp")
    width = weight.shape[2]
    groups = weight_hbm.shape[1] // width
    copies = []
    for i, offset in enumerate(offsets):
        start = pl.multiple_of(lax.rem(me + offset, groups) * width, width)
        copies.append(
            pltpu.make_async_copy(
                weight_hbm.at[:, pl.ds(start, width)], weight.at[i], sems.at[i]
            )
        )
    return copies


def project(attended, copies, weight, outs):
    for i, (copy, out_ref) in enumerate(zip(copies, outs)):
        copy.wait()
        out_ref[...] = jnp.dot(attended, weight[i], preferred_element_type=jnp.float32).astype(
            jnp.bfloat16
        )


def attend_kernel(
    steps,
    lengths_ref,
    bits_ref,
    got_ref,
    keys,
    values_hbm,
    weight_hbm,
    out_ref,
    far_ref,
    right_ref,
    left_ref,
    values,
    weight,
    here,
    cache_scores,
    fresh_scores,
    cache_weights,
    fresh_weights,
    inverse,
    value_sem,
    weight_sems,
):
    value_copy = pltpu.make_async_copy(values_hbm, values, value_sem)
    value_copy.start()
    copies = column_copies(FIRST, weight_hbm, weight, weight_sems)
    for copy in copies:
        copy.start()
    rows, context, head_size = keys.shape
    features = out_ref.shape[1]
    heads = features // head_size
    pair = 2 * steps
    lines = heads * pair
    scale = 1.0 / math.sqrt(head_size) * math.log2(math.e)
    here[...] = take_back(spots_matrix(bits_ref[...], steps), got_ref[...])

    upper = lax.broadcasted_iota(jnp.int32, (lines, context), 0) % pair < steps
    column = lax.broadcasted_iota(jnp.int32, (lines, context), 1)
    fresh_line = lax.broadcasted_iota(jnp.int32, (lines, pair), 0) % pair
    fresh_column = lax.broadcasted_iota(jnp.int32, (lines, pair), 1)
    fresh_live = (fresh_line // steps == fresh_column // steps) & (fresh_column <= fresh_line)
    out_upper = lax.broadcasted_iota(jnp.int32, (lines, head_size), 0) % pair < steps

    def score(left, right):
        return lax.dot_general(
            left, right, (((1,), (1,)), ((), ())), preferred_element_type=jnp.float32
        )

    def mix(weights, block):
        return jnp.dot(weights, block, preferred_element_type=jnp.float32)

    for i in range(rows // 2):
        a, b = 2 * i, 2 * i + 1
        block = here[i * pair : (i + 1) * pair, :]
        queries = jnp.concatenate(
            [block[:, h * head_size : (h + 1) * head_size] for h in range(heads)], axis=0
        )
        limit = jnp.where(upper, lengths_ref[a], lengths_ref[b])
        scores = jnp.where(upper, score(queries, keys[a]), score(queries, keys[b]))
        cache_scores[i] = jnp.where(column < limit, scores * scale, MASKED)
        fresh = score(queries, block[:, features : features + head_size])
        fresh_scores[i] = jnp.where(fresh_live, fresh * scale, MASKED)

    for i in range(rows // 2):
        scores, fresh = cache_scores[i], fresh_scores[i]
        peak = jnp.maximum(
            jnp.max(scores, axis=1, keepdims=True), jnp.max(fresh, axis=1, keepdims=True)
        )
        weights = jnp.exp2(scores - peak).astype(jnp.bfloat16)
        weights_new = jnp.exp2(fresh - peak).astype(jnp.bfloat16)
        cache_weights[i] = weights
        fresh_weights[i] = weights_new
        total = jnp.sum(weights.astype(jnp.float32), axis=1, keepdims=True) + jnp.sum(
            weights_new.astype(jnp.float32), axis=1, keepdims=True
        )
        inverse[i] = jnp.broadcast_to(1.0 / total, (lines, head_size))

    value_copy.wait()
    for i in range(rows // 2):
        lot = slice(i * pair, (i + 1) * pair)
        weights = cache_weights[i]
        summed = jnp.where(out_upper, mix(weights, values[2 * i]), mix(weights, values[2 * i + 1]))
        summed = summed + mix(fresh_weights[i], here[lot, features + head_size :])
        result = (summed * inverse[i]).astype(jnp.bfloat16)
        for h in range(heads):
            out_ref[lot, h * head_size : (h + 1) * head_size] = result[h * pair : (h + 1) * pair]

    project(out_ref[...], copies, weight, (far_ref, right_ref, left_ref))


def project_kernel(offsets, steps, attended_ref, weight_hbm, *refs):
    outs, (weight, sems) = refs[:-2], refs[-2:]
    copies = column_copies(offsets, weight_hbm, weight, sems)
    for copy in copies:
        copy.start()
    project(attended_ref[...], copies, weight, outs)


def wide(ref):
    return ref[...].astype(jnp.float32)


def relay_kernel(steps, right_ref, left_ref, from_left, from_right, far_ref, right_out, left_out):
    even = lax.rem(lax.axis_index("tp"), 2) == 0
    far = wide(far_ref)
    none = jnp.zeros_like(far)
    right = wide(right_ref) + wide(from_left) + jnp.where(even, far, none)
    left = wide(left_ref) + wide(from_right) + jnp.where(even, none, far)
    right_out[...] = right.astype(jnp.bfloat16)
    left_out[...] = left.astype(jnp.bfloat16)


def merge_kernel(steps, bits_ref, *refs):
    parts, out_ref = refs[:-1], refs[-1]
    total = wide(parts[0])
    for part in parts[1:]:
        total = total + wide(part)
    hot = spots_matrix(bits_ref[...], steps)
    out_ref[...] = jnp.dot(
        hot, total.astype(jnp.bfloat16), preferred_element_type=jnp.float32
    ).astype(jnp.bfloat16)


def unpack_kernel(steps, bits_ref, got_ref, out_ref):
    out_ref[...] = take_back(spots_matrix(bits_ref[...], steps), got_ref[...]).reshape(
        out_ref.shape
    )


def on_device(
    cache_keys,
    cache_values,
    cache_lengths,
    dest_replica,
    dest_slot,
    queries,
    new_keys,
    new_values,
    out_weight,
):
    replicas = lax.axis_size("rep")
    groups = lax.axis_size("tp")
    rows, _, context, head_size = cache_keys.shape
    steps, features = queries.shape[1:]
    tokens = rows * steps
    width = out_weight.shape[1] // groups
    spots = replicas * 2 * steps
    bf16 = jnp.bfloat16

    def out(shape, dtype=bf16):
        return jax.ShapeDtypeStruct(shape, dtype)

    def kernel(body, out_shape, in_specs, out_specs=None, scratch=(), cost=None):
        return pl.pallas_call(
            lambda *refs: body(steps, *refs),
            out_shape=out_shape,
            in_specs=in_specs,
            out_specs=vmem_spec() if out_specs is None else out_specs,
            scratch_shapes=scratch,
            compiler_params=params(),
            cost_estimate=cost,
        )

    wire, bits = kernel(
        route_kernel,
        (out((replicas, tokens), jnp.int32), out((replicas, tokens), jnp.int32)),
        [hbm_spec()] * 2,
        (vmem_spec(), vmem_spec()),
        [
            pltpu.VMEM((1, rows), jnp.int32),
            pltpu.VMEM((1, rows), jnp.int32),
            pltpu.SemaphoreType.DMA((2,)),
        ],
    )(in_hbm(dest_replica.reshape(1, rows)), in_hbm(dest_slot.reshape(1, rows)))
    wire = lax.all_to_all(wire.reshape(replicas, 1, tokens), "rep", 0, 0, tiled=True)
    wire = wire.reshape(replicas, tokens)

    full = features + 2 * head_size
    moving = jnp.concatenate([queries, new_keys, new_values], axis=2).reshape(tokens, full)
    packed = kernel(pack_kernel, out((spots, full)), [vmem_spec()] * 2)(wire, moving)
    got = lax.all_to_all(packed.reshape(replicas, 2 * steps, full), "rep", 0, 0, tiled=True)

    lines = features // head_size * 2 * steps
    chunk = out((tokens, width))
    attended, far, to_right, to_left = kernel(
        attend_kernel,
        (out((tokens, features)), chunk, chunk, chunk),
        [smem_spec()] + [vmem_spec()] * 3 + [hbm_spec()] * 2,
        (vmem_spec(),) * 4,
        [
            pltpu.VMEM((rows, context, head_size), bf16),
            pltpu.VMEM((len(FIRST), features, width), bf16),
            pltpu.VMEM((tokens, full), bf16),
            pltpu.VMEM((rows // 2, lines, context), jnp.float32),
            pltpu.VMEM((rows // 2, lines, 2 * steps), jnp.float32),
            pltpu.VMEM((rows // 2, lines, context), bf16),
            pltpu.VMEM((rows // 2, lines, 2 * steps), bf16),
            pltpu.VMEM((rows // 2, lines, head_size), jnp.float32),
            pltpu.SemaphoreType.DMA(()),
            pltpu.SemaphoreType.DMA((len(FIRST),)),
        ],
    )(
        cache_lengths,
        bits,
        got.reshape(spots, full),
        cache_keys.reshape(rows, context, head_size),
        in_hbm(cache_values.reshape(rows, context, head_size)),
        in_hbm(out_weight),
    )

    def shift(block, by):
        return lax.ppermute(block, "tp", [(i, (i + by) % groups) for i in range(groups)])

    far = lax.ppermute(
        far, "tp", [(i, (i + (-2 if i % 2 else 2)) % groups) for i in range(groups)]
    )
    from_left, from_right = shift(to_right, 1), shift(to_left, -1)
    def projected(offsets):
        count = len(offsets)
        return kernel(
            lambda steps, *refs: project_kernel(offsets, steps, *refs),
            (chunk,) * count,
            [vmem_spec(), hbm_spec()],
            (vmem_spec(),) * count,
            [
                pltpu.VMEM((count, features, width), bf16),
                pltpu.SemaphoreType.DMA((count,)),
            ],
            pl.CostEstimate(
                flops=2 * count * tokens * features * width,
                bytes_accessed=2 * count * features * width,
                transcendentals=0,
            ),
        )(attended, in_hbm(out_weight))

    next_right, next_left, near_right, near_left = projected(SECOND)
    (own,) = projected(LAST)
    near_from_left, near_from_right = shift(near_right, 1), shift(near_left, -1)
    relay_right, relay_left = kernel(
        relay_kernel, (chunk, chunk), [vmem_spec()] * 5, (vmem_spec(),) * 2
    )(next_right, next_left, from_left, from_right, far)
    sum_from_left, sum_from_right = shift(relay_right, 2), shift(relay_left, -2)
    back = kernel(merge_kernel, out((spots, width)), [vmem_spec()] * 6)(
        bits, own, near_from_left, near_from_right, sum_from_left, sum_from_right
    )
    back = lax.all_to_all(back.reshape(replicas, 2 * steps, width), "rep", 0, 0, tiled=True)
    return kernel(unpack_kernel, out((rows, steps, width)), [vmem_spec()] * 2)(
        wire, back.reshape(spots, width)
    )


def solution(mesh):
    return jax.shard_map(
        on_device,
        mesh=mesh,
        in_specs=(
            P("rep", "tp", None, None),
            P("rep", "tp", None, None),
            P("rep"),
            P("rep"),
            P("rep"),
            P("rep", None, "tp"),
            P("rep", None, "tp"),
            P("rep", None, "tp"),
            P("tp", None),
        ),
        out_specs=P("rep", None, "tp"),
        check_vma=False,
    )
```

```python
import math

import jax
import jax.numpy as jnp
from jax import lax
from jax.experimental import pallas as pl
from jax.experimental.pallas import tpu as pltpu
from jax.sharding import PartitionSpec as P

MASKED = -1e30
FIRST = (3, 5)
SECOND = (4, 2, 6)
THIRD = (1, 7)
LAST = (0,)
VMEM_BYTES = 24 * 1024 * 1024


def vmem_spec():
    return pl.BlockSpec(memory_space=pltpu.VMEM)


def smem_spec():
    return pl.BlockSpec(memory_space=pltpu.SMEM)


def hbm_spec():
    return pl.BlockSpec(memory_space=pltpu.HBM)


def in_hbm(array):
    return pltpu.with_memory_space_constraint(array, pltpu.HBM)


def params():
    return pltpu.CompilerParams(vmem_limit_bytes=VMEM_BYTES)


def spots_matrix(bits, steps):
    replicas, tokens = bits.shape
    shape = (replicas, 2 * steps, tokens)
    spread = jnp.broadcast_to(bits[:, None, :], shape)
    within = lax.broadcasted_iota(jnp.int32, shape, 1)
    token = lax.broadcasted_iota(jnp.int32, shape, 2)
    bit = jnp.where(within < steps, spread & 1, spread >> 1)
    hot = jnp.where((token % steps) == (within % steps), bit, 0)
    return hot.astype(jnp.float32).astype(jnp.bfloat16).reshape(replicas * 2 * steps, tokens)


def route_kernel(steps, *refs):
    sources, (wire_ref, bits_ref, moving_ref) = refs[:5], refs[5:8]
    locals_, sems = refs[8:13], refs[13]
    target_ref, slot_ref, *blocks = locals_
    copies = [
        pltpu.make_async_copy(source, local, sems.at[i])
        for i, (source, local) in enumerate(zip(sources, locals_))
    ]
    for copy in copies:
        copy.start()
    replicas, tokens = wire_ref.shape
    rows = tokens // steps
    shape = (replicas, tokens)
    spread = lax.broadcasted_iota(jnp.int32, (rows, tokens), 1) // steps
    spread = spread == lax.broadcasted_iota(jnp.int32, (rows, tokens), 0)
    spread = spread.astype(jnp.float32).astype(jnp.bfloat16)
    for copy in copies[:2]:
        copy.wait()
    both = jnp.where(
        lax.broadcasted_iota(jnp.int32, (8, rows), 0) == 0, target_ref[...], slot_ref[...]
    )
    both = jnp.dot(
        both.astype(jnp.float32).astype(jnp.bfloat16), spread, preferred_element_type=jnp.float32
    ).astype(jnp.int32)
    replica = lax.broadcasted_iota(jnp.int32, shape, 0)
    row = lax.broadcasted_iota(jnp.int32, shape, 1) // steps
    mine = both[0:1] == replica
    first = jnp.min(jnp.where(mine, row, tokens), axis=1, keepdims=True)
    early = mine & (row == first)
    late = mine & (row != first)
    slots = jnp.broadcast_to(both[1:2], shape)
    early_slot = jnp.max(jnp.where(early, slots, -1), axis=1, keepdims=True)
    late_slot = jnp.max(jnp.where(late, slots, -1), axis=1, keepdims=True)
    bits_ref[...] = jnp.where(early, 1, 0) + jnp.where(late, 2, 0)
    wire_ref[...] = jnp.where(row == early_slot, 1, 0) + jnp.where(row == late_slot, 2, 0)
    at = 0
    for copy, block in zip(copies[2:], blocks):
        copy.wait()
        features = block.shape[2]
        moving_ref[:, at : at + features] = block[...].reshape(tokens, features)
        at += features


def pack_kernel(steps, bits_ref, rows_ref, out_ref):
    hot = spots_matrix(bits_ref[...], steps)
    out_ref[...] = jnp.dot(hot, rows_ref[...], preferred_element_type=jnp.float32).astype(
        jnp.bfloat16
    )


def take_back(hot, rows):
    return lax.dot_general(
        hot, rows, (((0,), (0,)), ((), ())), preferred_element_type=jnp.float32
    ).astype(jnp.bfloat16)


def column_copies(offsets, weight_hbm, weight, sems):
    me = lax.axis_index("tp")
    width = weight.shape[2]
    groups = weight_hbm.shape[1] // width
    copies = []
    for i, offset in enumerate(offsets):
        start = pl.multiple_of(lax.rem(me + offset, groups) * width, width)
        copies.append(
            pltpu.make_async_copy(
                weight_hbm.at[:, pl.ds(start, width)], weight.at[i], sems.at[i]
            )
        )
    return copies


def project(attended, copies, weight, outs):
    for i, (copy, out_ref) in enumerate(zip(copies, outs)):
        copy.wait()
        out_ref[...] = jnp.dot(attended, weight[i], preferred_element_type=jnp.float32).astype(
            jnp.bfloat16
        )


def attend_kernel(
    steps,
    lengths_ref,
    bits_ref,
    got_ref,
    keys,
    values_hbm,
    weight_hbm,
    out_ref,
    right_ref,
    left_ref,
    values,
    weight,
    here,
    cache_scores,
    fresh_scores,
    cache_weights,
    fresh_weights,
    inverse,
    value_sem,
    weight_sems,
):
    value_copy = pltpu.make_async_copy(values_hbm, values, value_sem)
    value_copy.start()
    copies = column_copies(FIRST, weight_hbm, weight, weight_sems)
    for copy in copies:
        copy.start()
    rows, context, head_size = keys.shape
    features = out_ref.shape[1]
    heads = features // head_size
    pair = 2 * steps
    lines = heads * pair
    scale = 1.0 / math.sqrt(head_size) * math.log2(math.e)
    here[...] = take_back(spots_matrix(bits_ref[...], steps), got_ref[...])

    upper = lax.broadcasted_iota(jnp.int32, (lines, context), 0) % pair < steps
    column = lax.broadcasted_iota(jnp.int32, (lines, context), 1)
    fresh_line = lax.broadcasted_iota(jnp.int32, (lines, pair), 0) % pair
    fresh_column = lax.broadcasted_iota(jnp.int32, (lines, pair), 1)
    fresh_live = (fresh_line // steps == fresh_column // steps) & (fresh_column <= fresh_line)
    out_upper = lax.broadcasted_iota(jnp.int32, (lines, head_size), 0) % pair < steps

    def score(left, right):
        return lax.dot_general(
            left, right, (((1,), (1,)), ((), ())), preferred_element_type=jnp.float32
        )

    def mix(weights, block):
        return jnp.dot(weights, block, preferred_element_type=jnp.float32)

    for i in range(rows // 2):
        a, b = 2 * i, 2 * i + 1
        block = here[i * pair : (i + 1) * pair, :]
        queries = jnp.concatenate(
            [block[:, h * head_size : (h + 1) * head_size] for h in range(heads)], axis=0
        )
        limit = jnp.where(upper, lengths_ref[a], lengths_ref[b])
        scores = jnp.where(upper, score(queries, keys[a]), score(queries, keys[b]))
        cache_scores[i] = jnp.where(column < limit, scores * scale, MASKED)
        fresh = score(queries, block[:, features : features + head_size])
        fresh_scores[i] = jnp.where(fresh_live, fresh * scale, MASKED)

    for i in range(rows // 2):
        scores, fresh = cache_scores[i], fresh_scores[i]
        peak = jnp.maximum(
            jnp.max(scores, axis=1, keepdims=True), jnp.max(fresh, axis=1, keepdims=True)
        )
        weights = jnp.exp2(scores - peak).astype(jnp.bfloat16)
        weights_new = jnp.exp2(fresh - peak).astype(jnp.bfloat16)
        cache_weights[i] = weights
        fresh_weights[i] = weights_new
        total = jnp.sum(weights.astype(jnp.float32), axis=1, keepdims=True) + jnp.sum(
            weights_new.astype(jnp.float32), axis=1, keepdims=True
        )
        inverse[i] = jnp.broadcast_to(1.0 / total, (lines, head_size))

    value_copy.wait()
    for i in range(rows // 2):
        lot = slice(i * pair, (i + 1) * pair)
        weights = cache_weights[i]
        summed = jnp.where(out_upper, mix(weights, values[2 * i]), mix(weights, values[2 * i + 1]))
        summed = summed + mix(fresh_weights[i], here[lot, features + head_size :])
        result = (summed * inverse[i]).astype(jnp.bfloat16)
        for h in range(heads):
            out_ref[lot, h * head_size : (h + 1) * head_size] = result[h * pair : (h + 1) * pair]

    project(out_ref[...], copies, weight, (right_ref, left_ref))


def project_kernel(offsets, steps, attended_ref, weight_ref, *outs):
    me = lax.axis_index("tp")
    width = outs[0].shape[1]
    groups = weight_ref.shape[1] // width
    for offset, out_ref in zip(offsets, outs):
        start = pl.multiple_of(lax.rem(me + offset, groups) * width, width)
        out_ref[...] = jnp.dot(
            attended_ref[...],
            weight_ref[:, pl.ds(start, width)],
            preferred_element_type=jnp.float32,
        ).astype(jnp.bfloat16)


def wide(ref):
    return ref[...].astype(jnp.float32)


def relay_kernel(steps, right_ref, left_ref, from_left, from_right, *refs):
    far, out_ref = refs[:-1], refs[-1]
    even = lax.rem(lax.axis_index("tp"), 2) == 0
    right = wide(right_ref) + wide(from_left)
    left = wide(left_ref) + wide(from_right)
    if far:
        total = jnp.where(even, right, left) + wide(far[0])
    else:
        total = jnp.where(even, left, right)
    out_ref[...] = total.astype(jnp.bfloat16)


def merge_kernel(steps, bits_ref, *refs):
    parts, out_ref = refs[:-1], refs[-1]
    total = wide(parts[0])
    for part in parts[1:]:
        total = total + wide(part)
    hot = spots_matrix(bits_ref[...], steps)
    out_ref[...] = jnp.dot(
        hot, total.astype(jnp.bfloat16), preferred_element_type=jnp.float32
    ).astype(jnp.bfloat16)


def unpack_kernel(steps, bits_ref, got_ref, out_ref):
    out_ref[...] = take_back(spots_matrix(bits_ref[...], steps), got_ref[...]).reshape(
        out_ref.shape
    )


def on_device(
    cache_keys,
    cache_values,
    cache_lengths,
    dest_replica,
    dest_slot,
    queries,
    new_keys,
    new_values,
    out_weight,
):
    replicas = lax.axis_size("rep")
    groups = lax.axis_size("tp")
    rows, _, context, head_size = cache_keys.shape
    steps, features = queries.shape[1:]
    tokens = rows * steps
    width = out_weight.shape[1] // groups
    spots = replicas * 2 * steps
    bf16 = jnp.bfloat16

    def out(shape, dtype=bf16):
        return jax.ShapeDtypeStruct(shape, dtype)

    def kernel(body, out_shape, in_specs, out_specs=None, scratch=(), cost=None):
        return pl.pallas_call(
            lambda *refs: body(steps, *refs),
            out_shape=out_shape,
            in_specs=in_specs,
            out_specs=vmem_spec() if out_specs is None else out_specs,
            scratch_shapes=scratch,
            compiler_params=params(),
            cost_estimate=cost,
        )

    full = features + 2 * head_size
    sources = (
        dest_replica.reshape(1, rows),
        dest_slot.reshape(1, rows),
        queries,
        new_keys,
        new_values,
    )
    wire, bits, moving = kernel(
        route_kernel,
        (
            out((replicas, tokens), jnp.int32),
            out((replicas, tokens), jnp.int32),
            out((tokens, full)),
        ),
        [hbm_spec()] * 5,
        (vmem_spec(),) * 3,
        [pltpu.VMEM(source.shape, source.dtype) for source in sources]
        + [pltpu.SemaphoreType.DMA((5,))],
    )(*(in_hbm(source) for source in sources))
    wire = lax.all_to_all(wire.reshape(replicas, 1, tokens), "rep", 0, 0, tiled=True)
    wire = wire.reshape(replicas, tokens)

    packed = kernel(pack_kernel, out((spots, full)), [vmem_spec()] * 2)(wire, moving)
    got = lax.all_to_all(packed.reshape(replicas, 2 * steps, full), "rep", 0, 0, tiled=True)

    lines = features // head_size * 2 * steps
    chunk = out((tokens, width))
    attended, to_right, to_left = kernel(
        attend_kernel,
        (out((tokens, features)), chunk, chunk),
        [smem_spec()] + [vmem_spec()] * 3 + [hbm_spec()] * 2,
        (vmem_spec(),) * 3,
        [
            pltpu.VMEM((rows, context, head_size), bf16),
            pltpu.VMEM((len(FIRST), features, width), bf16),
            pltpu.VMEM((tokens, full), bf16),
            pltpu.VMEM((rows // 2, lines, context), jnp.float32),
            pltpu.VMEM((rows // 2, lines, 2 * steps), jnp.float32),
            pltpu.VMEM((rows // 2, lines, context), bf16),
            pltpu.VMEM((rows // 2, lines, 2 * steps), bf16),
            pltpu.VMEM((rows // 2, lines, head_size), jnp.float32),
            pltpu.SemaphoreType.DMA(()),
            pltpu.SemaphoreType.DMA((len(FIRST),)),
        ],
    )(
        cache_lengths,
        bits,
        got.reshape(spots, full),
        cache_keys.reshape(rows, context, head_size),
        in_hbm(cache_values.reshape(rows, context, head_size)),
        in_hbm(out_weight),
    )

    def shift(block, by):
        return lax.ppermute(block, "tp", [(i, (i + by) % groups) for i in range(groups)])

    def cross(block, by):
        return lax.ppermute(
            block, "tp", [(i, (i + (-by if i % 2 else by)) % groups) for i in range(groups)]
        )

    from_left, from_right = shift(to_right, 1), shift(to_left, -1)
    def projected(offsets):
        count = len(offsets)
        return kernel(
            lambda steps, *refs: project_kernel(offsets, steps, *refs),
            (chunk,) * count,
            [vmem_spec()] * 2,
            (vmem_spec(),) * count,
            (),
            pl.CostEstimate(
                flops=2 * count * tokens * features * width,
                bytes_accessed=2 * count * features * width,
                transcendentals=0,
            ),
        )(attended, out_weight)

    far, next_right, next_left = projected(SECOND)
    far = cross(far, 2)
    near_right, near_left = projected(THIRD)
    (own,) = projected(LAST)
    inner = (next_right, next_left, from_left, from_right)
    relay = [
        kernel(relay_kernel, chunk, [vmem_spec()] * len(blocks))(*blocks)
        for blocks in (inner, (*inner, far))
    ]
    first = cross(relay[0], -2)
    near_from_left, near_from_right = shift(near_right, 1), shift(near_left, -1)
    second = cross(relay[1], 2)
    back = kernel(merge_kernel, out((spots, width)), [vmem_spec()] * 6)(
        bits, own, near_from_left, near_from_right, first, second
    )
    back = lax.all_to_all(back.reshape(replicas, 2 * steps, width), "rep", 0, 0, tiled=True)
    return kernel(unpack_kernel, out((rows, steps, width)), [vmem_spec()] * 2)(
        wire, back.reshape(spots, width)
    )


def solution(mesh):
    return jax.shard_map(
        on_device,
        mesh=mesh,
        in_specs=(
            P("rep", "tp", None, None),
            P("rep", "tp", None, None),
            P("rep"),
            P("rep"),
            P("rep"),
            P("rep", None, "tp"),
            P("rep", None, "tp"),
            P("rep", None, "tp"),
            P("tp", None),
        ),
        out_specs=P("rep", None, "tp"),
        check_vma=False,
    )
```

```python
import math

import jax
import jax.numpy as jnp
from jax import lax
from jax.experimental import pallas as pl
from jax.experimental.pallas import tpu as pltpu
from jax.sharding import PartitionSpec as P

MASKED = -1e30
FIRST = ((3, 5),)
SECOND = (4, (6, 2))
THIRD = ((1, 7),)
LAST = (0,)
VMEM_BYTES = 24 * 1024 * 1024


def vmem_spec():
    return pl.BlockSpec(memory_space=pltpu.VMEM)


def smem_spec():
    return pl.BlockSpec(memory_space=pltpu.SMEM)


def hbm_spec():
    return pl.BlockSpec(memory_space=pltpu.HBM)


def in_hbm(array):
    return pltpu.with_memory_space_constraint(array, pltpu.HBM)


def params():
    return pltpu.CompilerParams(vmem_limit_bytes=VMEM_BYTES)


def spots_matrix(bits, steps):
    replicas, tokens = bits.shape
    shape = (replicas, 2 * steps, tokens)
    spread = jnp.broadcast_to(bits[:, None, :], shape)
    within = lax.broadcasted_iota(jnp.int32, shape, 1)
    token = lax.broadcasted_iota(jnp.int32, shape, 2)
    bit = jnp.where(within < steps, spread & 1, spread >> 1)
    hot = jnp.where((token % steps) == (within % steps), bit, 0)
    return hot.astype(jnp.float32).astype(jnp.bfloat16).reshape(replicas * 2 * steps, tokens)


def route_kernel(steps, *refs):
    sources, (wire_ref, bits_ref, moving_ref) = refs[:5], refs[5:8]
    locals_, sems = refs[8:13], refs[13]
    target_ref, slot_ref, *blocks = locals_
    copies = [
        pltpu.make_async_copy(source, local, sems.at[i])
        for i, (source, local) in enumerate(zip(sources, locals_))
    ]
    for copy in copies:
        copy.start()
    replicas, tokens = wire_ref.shape
    rows = tokens // steps
    shape = (replicas, tokens)
    spread = lax.broadcasted_iota(jnp.int32, (rows, tokens), 1) // steps
    spread = spread == lax.broadcasted_iota(jnp.int32, (rows, tokens), 0)
    spread = spread.astype(jnp.float32).astype(jnp.bfloat16)
    for copy in copies[:2]:
        copy.wait()
    both = jnp.where(
        lax.broadcasted_iota(jnp.int32, (8, rows), 0) == 0, target_ref[...], slot_ref[...]
    )
    both = jnp.dot(
        both.astype(jnp.float32).astype(jnp.bfloat16), spread, preferred_element_type=jnp.float32
    ).astype(jnp.int32)
    replica = lax.broadcasted_iota(jnp.int32, shape, 0)
    row = lax.broadcasted_iota(jnp.int32, shape, 1) // steps
    mine = both[0:1] == replica
    first = jnp.min(jnp.where(mine, row, tokens), axis=1, keepdims=True)
    early = mine & (row == first)
    late = mine & (row != first)
    slots = jnp.broadcast_to(both[1:2], shape)
    early_slot = jnp.max(jnp.where(early, slots, -1), axis=1, keepdims=True)
    late_slot = jnp.max(jnp.where(late, slots, -1), axis=1, keepdims=True)
    bits_ref[...] = jnp.where(early, 1, 0) + jnp.where(late, 2, 0)
    wire_ref[...] = jnp.where(row == early_slot, 1, 0) + jnp.where(row == late_slot, 2, 0)
    at = 0
    for copy, block in zip(copies[2:], blocks):
        copy.wait()
        features = block.shape[2]
        moving_ref[:, at : at + features] = block[...].reshape(tokens, features)
        at += features


def pack_kernel(steps, bits_ref, rows_ref, out_ref):
    hot = spots_matrix(bits_ref[...], steps)
    out_ref[...] = jnp.dot(hot, rows_ref[...], preferred_element_type=jnp.float32).astype(
        jnp.bfloat16
    )


def take_back(hot, rows):
    return lax.dot_general(
        hot, rows, (((0,), (0,)), ((), ())), preferred_element_type=jnp.float32
    ).astype(jnp.bfloat16)


def column_start(offset, groups, width):
    return pl.multiple_of(lax.rem(lax.axis_index("tp") + offset, groups) * width, width)


def flat(chunks):
    return [offset for chunk in chunks for offset in (chunk if isinstance(chunk, tuple) else [chunk])]


def give_out(chunks, products, outs):
    odd = (lax.axis_index("tp") & 1) == 1
    products, outs = iter(products), iter(outs)
    for chunk in chunks:
        if isinstance(chunk, tuple):
            one, other = next(products), next(products)
            next(outs)[...] = jnp.where(odd, one, other)
            next(outs)[...] = jnp.where(odd, other, one)
        else:
            next(outs)[...] = next(products)


def project(attended, columns):
    return jnp.dot(attended, columns, preferred_element_type=jnp.float32).astype(jnp.bfloat16)


def attend_kernel(
    steps,
    lengths_ref,
    bits_ref,
    got_ref,
    keys,
    values_hbm,
    weight_hbm,
    out_ref,
    outer_ref,
    inner_ref,
    values,
    weight,
    here,
    cache_scores,
    fresh_scores,
    cache_weights,
    fresh_weights,
    inverse,
    value_sem,
    weight_sems,
):
    value_copy = pltpu.make_async_copy(values_hbm, values, value_sem)
    value_copy.start()
    width = outer_ref.shape[1]
    groups = weight_hbm.shape[1] // width
    copies = [
        pltpu.make_async_copy(
            weight_hbm.at[:, pl.ds(column_start(offset, groups, width), width)],
            weight.at[i],
            weight_sems.at[i],
        )
        for i, offset in enumerate(flat(FIRST))
    ]
    for copy in copies:
        copy.start()
    rows, context, head_size = keys.shape
    features = out_ref.shape[1]
    heads = features // head_size
    pair = 2 * steps
    lines = heads * pair
    scale = 1.0 / math.sqrt(head_size) * math.log2(math.e)
    here[...] = take_back(spots_matrix(bits_ref[...], steps), got_ref[...])

    upper = lax.broadcasted_iota(jnp.int32, (lines, context), 0) % pair < steps
    column = lax.broadcasted_iota(jnp.int32, (lines, context), 1)
    fresh_line = lax.broadcasted_iota(jnp.int32, (lines, pair), 0) % pair
    fresh_column = lax.broadcasted_iota(jnp.int32, (lines, pair), 1)
    fresh_live = (fresh_line // steps == fresh_column // steps) & (fresh_column <= fresh_line)
    out_upper = lax.broadcasted_iota(jnp.int32, (lines, head_size), 0) % pair < steps

    def score(left, right):
        return lax.dot_general(
            left, right, (((1,), (1,)), ((), ())), preferred_element_type=jnp.float32
        )

    def mix(weights, block):
        return jnp.dot(weights, block, preferred_element_type=jnp.float32)

    for i in range(rows // 2):
        a, b = 2 * i, 2 * i + 1
        block = here[i * pair : (i + 1) * pair, :]
        queries = jnp.concatenate(
            [block[:, h * head_size : (h + 1) * head_size] for h in range(heads)], axis=0
        )
        limit = jnp.where(upper, lengths_ref[a], lengths_ref[b])
        scores = jnp.where(upper, score(queries, keys[a]), score(queries, keys[b]))
        cache_scores[i] = jnp.where(column < limit, scores * scale, MASKED)
        fresh = score(queries, block[:, features : features + head_size])
        fresh_scores[i] = jnp.where(fresh_live, fresh * scale, MASKED)

    for i in range(rows // 2):
        scores, fresh = cache_scores[i], fresh_scores[i]
        peak = jnp.maximum(
            jnp.max(scores, axis=1, keepdims=True), jnp.max(fresh, axis=1, keepdims=True)
        )
        weights = jnp.exp2(scores - peak).astype(jnp.bfloat16)
        weights_new = jnp.exp2(fresh - peak).astype(jnp.bfloat16)
        cache_weights[i] = weights
        fresh_weights[i] = weights_new
        total = jnp.sum(weights.astype(jnp.float32), axis=1, keepdims=True) + jnp.sum(
            weights_new.astype(jnp.float32), axis=1, keepdims=True
        )
        inverse[i] = jnp.broadcast_to(1.0 / total, (lines, head_size))

    value_copy.wait()
    for i in range(rows // 2):
        lot = slice(i * pair, (i + 1) * pair)
        weights = cache_weights[i]
        summed = jnp.where(out_upper, mix(weights, values[2 * i]), mix(weights, values[2 * i + 1]))
        summed = summed + mix(fresh_weights[i], here[lot, features + head_size :])
        result = (summed * inverse[i]).astype(jnp.bfloat16)
        for h in range(heads):
            out_ref[lot, h * head_size : (h + 1) * head_size] = result[h * pair : (h + 1) * pair]

    products = []
    for i, copy in enumerate(copies):
        copy.wait()
        products.append(project(out_ref[...], weight[i]))
    give_out(FIRST, products, (outer_ref, inner_ref))


def project_kernel(chunks, steps, attended_ref, weight_ref, *outs):
    width = outs[0].shape[1]
    groups = weight_ref.shape[1] // width
    products = [
        project(attended_ref[...], weight_ref[:, pl.ds(column_start(offset, groups, width), width)])
        for offset in flat(chunks)
    ]
    give_out(chunks, products, outs)


def wide(ref):
    return ref[...].astype(jnp.float32)


def relay_kernel(steps, *refs):
    total = wide(refs[0])
    for ref in refs[1:-1]:
        total = total + wide(ref)
    refs[-1][...] = total.astype(jnp.bfloat16)


def merge_kernel(steps, bits_ref, *refs):
    parts, out_ref = refs[:-1], refs[-1]
    total = wide(parts[0])
    for part in parts[1:]:
        total = total + wide(part)
    hot = spots_matrix(bits_ref[...], steps)
    out_ref[...] = jnp.dot(
        hot, total.astype(jnp.bfloat16), preferred_element_type=jnp.float32
    ).astype(jnp.bfloat16)


def unpack_kernel(steps, bits_ref, got_ref, out_ref):
    out_ref[...] = take_back(spots_matrix(bits_ref[...], steps), got_ref[...]).reshape(
        out_ref.shape
    )


def on_device(
    cache_keys,
    cache_values,
    cache_lengths,
    dest_replica,
    dest_slot,
    queries,
    new_keys,
    new_values,
    out_weight,
):
    replicas = lax.axis_size("rep")
    groups = lax.axis_size("tp")
    rows, _, context, head_size = cache_keys.shape
    steps, features = queries.shape[1:]
    tokens = rows * steps
    width = out_weight.shape[1] // groups
    spots = replicas * 2 * steps
    bf16 = jnp.bfloat16

    def out(shape, dtype=bf16):
        return jax.ShapeDtypeStruct(shape, dtype)

    def kernel(body, out_shape, in_specs, out_specs=None, scratch=(), cost=None):
        return pl.pallas_call(
            lambda *refs: body(steps, *refs),
            out_shape=out_shape,
            in_specs=in_specs,
            out_specs=vmem_spec() if out_specs is None else out_specs,
            scratch_shapes=scratch,
            compiler_params=params(),
            cost_estimate=cost,
        )

    full = features + 2 * head_size
    sources = (
        dest_replica.reshape(1, rows),
        dest_slot.reshape(1, rows),
        queries,
        new_keys,
        new_values,
    )
    wire, bits, moving = kernel(
        route_kernel,
        (
            out((replicas, tokens), jnp.int32),
            out((replicas, tokens), jnp.int32),
            out((tokens, full)),
        ),
        [hbm_spec()] * 5,
        (vmem_spec(),) * 3,
        [pltpu.VMEM(source.shape, source.dtype) for source in sources]
        + [pltpu.SemaphoreType.DMA((5,))],
    )(*(in_hbm(source) for source in sources))
    wire = lax.all_to_all(wire.reshape(replicas, 1, tokens), "rep", 0, 0, tiled=True)
    wire = wire.reshape(replicas, tokens)

    packed = kernel(pack_kernel, out((spots, full)), [vmem_spec()] * 2)(wire, moving)
    got = lax.all_to_all(packed.reshape(replicas, 2 * steps, full), "rep", 0, 0, tiled=True)

    lines = features // head_size * 2 * steps
    chunk = out((tokens, width))
    attended, outer, inner = kernel(
        attend_kernel,
        (out((tokens, features)), chunk, chunk),
        [smem_spec()] + [vmem_spec()] * 3 + [hbm_spec()] * 2,
        (vmem_spec(),) * 3,
        [
            pltpu.VMEM((rows, context, head_size), bf16),
            pltpu.VMEM((len(flat(FIRST)), features, width), bf16),
            pltpu.VMEM((tokens, full), bf16),
            pltpu.VMEM((rows // 2, lines, context), jnp.float32),
            pltpu.VMEM((rows // 2, lines, 2 * steps), jnp.float32),
            pltpu.VMEM((rows // 2, lines, context), bf16),
            pltpu.VMEM((rows // 2, lines, 2 * steps), bf16),
            pltpu.VMEM((rows // 2, lines, head_size), jnp.float32),
            pltpu.SemaphoreType.DMA(()),
            pltpu.SemaphoreType.DMA((len(flat(FIRST)),)),
        ],
    )(
        cache_lengths,
        bits,
        got.reshape(spots, full),
        cache_keys.reshape(rows, context, head_size),
        in_hbm(cache_values.reshape(rows, context, head_size)),
        in_hbm(out_weight),
    )

    def cross(block, by):
        return lax.ppermute(
            block, "tp", [(i, (i + (by if i % 2 else -by)) % groups) for i in range(groups)]
        )

    outer, inner = cross(outer, 1), cross(inner, -1)

    def projected(chunks):
        count = len(flat(chunks))
        return kernel(
            lambda steps, *refs: project_kernel(chunks, steps, *refs),
            (chunk,) * count,
            [vmem_spec()] * 2,
            (vmem_spec(),) * count,
            (),
            pl.CostEstimate(
                flops=2 * count * tokens * features * width,
                bytes_accessed=2 * count * features * width,
                transcendentals=0,
            ),
        )(attended, out_weight)

    far, first, second = projected(SECOND)
    far = cross(far, 2)
    near = [cross(block, by) for block, by in zip(projected(THIRD), (1, -1))]
    (own,) = projected(LAST)

    def relay(*blocks):
        return kernel(relay_kernel, chunk, [vmem_spec()] * len(blocks))(*blocks)

    first = cross(relay(first, outer), -2)
    second = cross(relay(second, inner, far), 2)
    back = kernel(merge_kernel, out((spots, width)), [vmem_spec()] * 6)(
        bits, own, *near, first, second
    )
    back = lax.all_to_all(back.reshape(replicas, 2 * steps, width), "rep", 0, 0, tiled=True)
    return kernel(unpack_kernel, out((rows, steps, width)), [vmem_spec()] * 2)(
        wire, back.reshape(spots, width)
    )


def solution(mesh):
    return jax.shard_map(
        on_device,
        mesh=mesh,
        in_specs=(
            P("rep", "tp", None, None),
            P("rep", "tp", None, None),
            P("rep"),
            P("rep"),
            P("rep"),
            P("rep", None, "tp"),
            P("rep", None, "tp"),
            P("rep", None, "tp"),
            P("tp", None),
        ),
        out_specs=P("rep", None, "tp"),
        check_vma=False,
    )
```

```python
import math

import jax
import jax.numpy as jnp
from jax import lax
from jax.experimental import pallas as pl
from jax.experimental.pallas import tpu as pltpu
from jax.sharding import PartitionSpec as P

MASKED = -1e30
FIRST = ((3, 5),)
SECOND = (4, (6, 2))
THIRD = ((1, 7),)
LAST = (0,)
VMEM_BYTES = 24 * 1024 * 1024


def vmem_spec():
    return pl.BlockSpec(memory_space=pltpu.VMEM)


def smem_spec():
    return pl.BlockSpec(memory_space=pltpu.SMEM)


def hbm_spec():
    return pl.BlockSpec(memory_space=pltpu.HBM)


def in_hbm(array):
    return pltpu.with_memory_space_constraint(array, pltpu.HBM)


def params():
    return pltpu.CompilerParams(vmem_limit_bytes=VMEM_BYTES)


def spots_matrix(bits, steps):
    replicas, tokens = bits.shape
    shape = (replicas, 2 * steps, tokens)
    spread = jnp.broadcast_to(bits[:, None, :], shape)
    within = lax.broadcasted_iota(jnp.int32, shape, 1)
    token = lax.broadcasted_iota(jnp.int32, shape, 2)
    bit = jnp.where(within < steps, spread & 1, spread >> 1)
    hot = jnp.where((token % steps) == (within % steps), bit, 0)
    return hot.astype(jnp.float32).astype(jnp.bfloat16).reshape(replicas * 2 * steps, tokens)


def route_kernel(steps, *refs):
    sources, (wire_ref, bits_ref, moving_ref) = refs[:5], refs[5:8]
    locals_, sems = refs[8:13], refs[13]
    target_ref, slot_ref, *blocks = locals_
    copies = [
        pltpu.make_async_copy(source, local, sems.at[i])
        for i, (source, local) in enumerate(zip(sources, locals_))
    ]
    for copy in copies:
        copy.start()
    replicas, tokens = wire_ref.shape
    rows = tokens // steps
    shift = rows.bit_length()
    replica = lax.broadcasted_iota(jnp.int32, (replicas, rows), 0)
    order = lax.broadcasted_iota(jnp.int32, (replicas, rows), 1) << shift
    row = lax.broadcasted_iota(jnp.int32, (replicas, tokens), 1) // steps
    for copy in copies[:2]:
        copy.wait()
    mine = target_ref[...] == replica
    key = order + slot_ref[...]
    early = jnp.min(jnp.where(mine, key, (1 << 24) - 1), axis=1, keepdims=True)
    late = jnp.max(jnp.where(mine, key, -1), axis=1, keepdims=True)
    low = (1 << shift) - 1
    wire_ref[...] = jnp.where(row == (early & low), 1, 0) + jnp.where(row == (late & low), 2, 0)
    bits_ref[...] = jnp.where(row == (early >> shift), 1, 0) + jnp.where(row == (late >> shift), 2, 0)
    at = 0
    for copy, block in zip(copies[2:], blocks):
        copy.wait()
        features = block.shape[2]
        moving_ref[:, at : at + features] = block[...].reshape(tokens, features)
        at += features


def pack_kernel(steps, bits_ref, rows_ref, out_ref):
    hot = spots_matrix(bits_ref[...], steps)
    out_ref[...] = jnp.dot(hot, rows_ref[...], preferred_element_type=jnp.float32).astype(
        jnp.bfloat16
    )


def take_back(hot, rows):
    return lax.dot_general(
        hot, rows, (((0,), (0,)), ((), ())), preferred_element_type=jnp.float32
    ).astype(jnp.bfloat16)


def column_start(offset, groups, width):
    return pl.multiple_of(lax.rem(lax.axis_index("tp") + offset, groups) * width, width)


def flat(chunks):
    return [offset for chunk in chunks for offset in (chunk if isinstance(chunk, tuple) else [chunk])]


def give_out(chunks, products, outs):
    odd = (lax.axis_index("tp") & 1) == 1
    products, outs = iter(products), iter(outs)
    for chunk in chunks:
        if isinstance(chunk, tuple):
            one, other = next(products), next(products)
            next(outs)[...] = jnp.where(odd, one, other)
            next(outs)[...] = jnp.where(odd, other, one)
        else:
            next(outs)[...] = next(products)


def project(attended, columns):
    return jnp.dot(attended, columns, preferred_element_type=jnp.float32).astype(jnp.bfloat16)


def attend_kernel(
    steps,
    lengths_ref,
    bits_ref,
    got_ref,
    keys,
    values_hbm,
    weight_hbm,
    out_ref,
    outer_ref,
    inner_ref,
    values,
    weight,
    here,
    cache_scores,
    fresh_scores,
    cache_weights,
    fresh_weights,
    inverse,
    value_sem,
    weight_sems,
):
    value_copy = pltpu.make_async_copy(values_hbm, values, value_sem)
    value_copy.start()
    width = outer_ref.shape[1]
    groups = weight_hbm.shape[1] // width
    copies = [
        pltpu.make_async_copy(
            weight_hbm.at[:, pl.ds(column_start(offset, groups, width), width)],
            weight.at[i],
            weight_sems.at[i],
        )
        for i, offset in enumerate(flat(FIRST))
    ]
    for copy in copies:
        copy.start()
    rows, context, head_size = keys.shape
    features = out_ref.shape[1]
    heads = features // head_size
    pair = 2 * steps
    lines = heads * pair
    scale = 1.0 / math.sqrt(head_size) * math.log2(math.e)
    here[...] = take_back(spots_matrix(bits_ref[...], steps), got_ref[...])

    upper = lax.broadcasted_iota(jnp.int32, (lines, context), 0) % pair < steps
    column = lax.broadcasted_iota(jnp.int32, (lines, context), 1)
    fresh_line = lax.broadcasted_iota(jnp.int32, (lines, pair), 0) % pair
    fresh_column = lax.broadcasted_iota(jnp.int32, (lines, pair), 1)
    fresh_live = (fresh_line // steps == fresh_column // steps) & (fresh_column <= fresh_line)
    out_upper = lax.broadcasted_iota(jnp.int32, (lines, head_size), 0) % pair < steps

    def score(left, right):
        return lax.dot_general(
            left, right, (((1,), (1,)), ((), ())), preferred_element_type=jnp.float32
        )

    def mix(weights, block):
        return jnp.dot(weights, block, preferred_element_type=jnp.float32)

    for i in range(rows // 2):
        a, b = 2 * i, 2 * i + 1
        block = here[i * pair : (i + 1) * pair, :]
        queries = jnp.concatenate(
            [block[:, h * head_size : (h + 1) * head_size] for h in range(heads)], axis=0
        )
        limit = jnp.where(upper, lengths_ref[a], lengths_ref[b])
        scores = jnp.where(upper, score(queries, keys[a]), score(queries, keys[b]))
        cache_scores[i] = jnp.where(column < limit, scores * scale, MASKED)
        fresh = score(queries, block[:, features : features + head_size])
        fresh_scores[i] = jnp.where(fresh_live, fresh * scale, MASKED)

    for i in range(rows // 2):
        scores, fresh = cache_scores[i], fresh_scores[i]
        peak = jnp.maximum(
            jnp.max(scores, axis=1, keepdims=True), jnp.max(fresh, axis=1, keepdims=True)
        )
        weights = jnp.exp2(scores - peak).astype(jnp.bfloat16)
        weights_new = jnp.exp2(fresh - peak).astype(jnp.bfloat16)
        cache_weights[i] = weights
        fresh_weights[i] = weights_new
        total = jnp.sum(weights.astype(jnp.float32), axis=1, keepdims=True) + jnp.sum(
            weights_new.astype(jnp.float32), axis=1, keepdims=True
        )
        inverse[i] = jnp.broadcast_to(1.0 / total, (lines, head_size))

    value_copy.wait()
    for i in range(rows // 2):
        lot = slice(i * pair, (i + 1) * pair)
        weights = cache_weights[i]
        summed = jnp.where(out_upper, mix(weights, values[2 * i]), mix(weights, values[2 * i + 1]))
        summed = summed + mix(fresh_weights[i], here[lot, features + head_size :])
        result = (summed * inverse[i]).astype(jnp.bfloat16)
        for h in range(heads):
            out_ref[lot, h * head_size : (h + 1) * head_size] = result[h * pair : (h + 1) * pair]

    products = []
    for i, copy in enumerate(copies):
        copy.wait()
        products.append(project(out_ref[...], weight[i]))
    give_out(FIRST, products, (outer_ref, inner_ref))


def project_kernel(chunks, steps, attended_ref, weight_ref, *outs):
    width = outs[0].shape[1]
    groups = weight_ref.shape[1] // width
    products = [
        project(attended_ref[...], weight_ref[:, pl.ds(column_start(offset, groups, width), width)])
        for offset in flat(chunks)
    ]
    give_out(chunks, products, outs)


def wide(ref):
    return ref[...].astype(jnp.float32)


def relay_kernel(steps, *refs):
    total = wide(refs[0])
    for ref in refs[1:-1]:
        total = total + wide(ref)
    refs[-1][...] = total.astype(jnp.bfloat16)


def merge_kernel(steps, bits_ref, *refs):
    parts, out_ref = refs[:-1], refs[-1]
    total = wide(parts[0])
    for part in parts[1:]:
        total = total + wide(part)
    hot = spots_matrix(bits_ref[...], steps)
    out_ref[...] = jnp.dot(
        hot, total.astype(jnp.bfloat16), preferred_element_type=jnp.float32
    ).astype(jnp.bfloat16)


def unpack_kernel(steps, bits_ref, got_ref, out_ref):
    out_ref[...] = take_back(spots_matrix(bits_ref[...], steps), got_ref[...]).reshape(
        out_ref.shape
    )


def on_device(
    cache_keys,
    cache_values,
    cache_lengths,
    dest_replica,
    dest_slot,
    queries,
    new_keys,
    new_values,
    out_weight,
):
    replicas = lax.axis_size("rep")
    groups = lax.axis_size("tp")
    rows, _, context, head_size = cache_keys.shape
    steps, features = queries.shape[1:]
    tokens = rows * steps
    width = out_weight.shape[1] // groups
    spots = replicas * 2 * steps
    bf16 = jnp.bfloat16

    def out(shape, dtype=bf16):
        return jax.ShapeDtypeStruct(shape, dtype)

    def kernel(body, out_shape, in_specs, out_specs=None, scratch=(), cost=None):
        return pl.pallas_call(
            lambda *refs: body(steps, *refs),
            out_shape=out_shape,
            in_specs=in_specs,
            out_specs=vmem_spec() if out_specs is None else out_specs,
            scratch_shapes=scratch,
            compiler_params=params(),
            cost_estimate=cost,
        )

    full = features + 2 * head_size
    sources = (
        dest_replica.reshape(1, rows),
        dest_slot.reshape(1, rows),
        queries,
        new_keys,
        new_values,
    )
    wire, bits, moving = kernel(
        route_kernel,
        (
            out((replicas, tokens), jnp.int32),
            out((replicas, tokens), jnp.int32),
            out((tokens, full)),
        ),
        [hbm_spec()] * 5,
        (vmem_spec(),) * 3,
        [pltpu.VMEM(source.shape, source.dtype) for source in sources]
        + [pltpu.SemaphoreType.DMA((5,))],
    )(*(in_hbm(source) for source in sources))
    wire = lax.all_to_all(wire.reshape(replicas, 1, tokens), "rep", 0, 0, tiled=True)
    wire = wire.reshape(replicas, tokens)

    packed = kernel(pack_kernel, out((spots, full)), [vmem_spec()] * 2)(wire, moving)
    got = lax.all_to_all(packed.reshape(replicas, 2 * steps, full), "rep", 0, 0, tiled=True)

    lines = features // head_size * 2 * steps
    chunk = out((tokens, width))
    attended, outer, inner = kernel(
        attend_kernel,
        (out((tokens, features)), chunk, chunk),
        [smem_spec()] + [vmem_spec()] * 3 + [hbm_spec()] * 2,
        (vmem_spec(),) * 3,
        [
            pltpu.VMEM((rows, context, head_size), bf16),
            pltpu.VMEM((len(flat(FIRST)), features, width), bf16),
            pltpu.VMEM((tokens, full), bf16),
            pltpu.VMEM((rows // 2, lines, context), jnp.float32),
            pltpu.VMEM((rows // 2, lines, 2 * steps), jnp.float32),
            pltpu.VMEM((rows // 2, lines, context), bf16),
            pltpu.VMEM((rows // 2, lines, 2 * steps), bf16),
            pltpu.VMEM((rows // 2, lines, head_size), jnp.float32),
            pltpu.SemaphoreType.DMA(()),
            pltpu.SemaphoreType.DMA((len(flat(FIRST)),)),
        ],
    )(
        cache_lengths,
        bits,
        got.reshape(spots, full),
        cache_keys.reshape(rows, context, head_size),
        in_hbm(cache_values.reshape(rows, context, head_size)),
        in_hbm(out_weight),
    )

    def cross(block, by):
        return lax.ppermute(
            block, "tp", [(i, (i + (by if i % 2 else -by)) % groups) for i in range(groups)]
        )

    outer, inner = cross(outer, 1), cross(inner, -1)

    def projected(chunks):
        count = len(flat(chunks))
        return kernel(
            lambda steps, *refs: project_kernel(chunks, steps, *refs),
            (chunk,) * count,
            [vmem_spec()] * 2,
            (vmem_spec(),) * count,
            (),
            pl.CostEstimate(
                flops=2 * count * tokens * features * width,
                bytes_accessed=2 * count * features * width,
                transcendentals=0,
            ),
        )(attended, out_weight)

    far, first, second = projected(SECOND)
    far = cross(far, 2)
    near = [cross(block, by) for block, by in zip(projected(THIRD), (1, -1))]
    (own,) = projected(LAST)

    def relay(*blocks):
        return kernel(relay_kernel, chunk, [vmem_spec()] * len(blocks))(*blocks)

    first = cross(relay(first, outer), -2)
    second = cross(relay(second, inner, far), 2)
    back = kernel(merge_kernel, out((spots, width)), [vmem_spec()] * 6)(
        bits, own, *near, first, second
    )
    back = lax.all_to_all(back.reshape(replicas, 2 * steps, width), "rep", 0, 0, tiled=True)
    return kernel(unpack_kernel, out((rows, steps, width)), [vmem_spec()] * 2)(
        wire, back.reshape(spots, width)
    )


def solution(mesh):
    return jax.shard_map(
        on_device,
        mesh=mesh,
        in_specs=(
            P("rep", "tp", None, None),
            P("rep", "tp", None, None),
            P("rep"),
            P("rep"),
            P("rep"),
            P("rep", None, "tp"),
            P("rep", None, "tp"),
            P("rep", None, "tp"),
            P("tp", None),
        ),
        out_specs=P("rep", None, "tp"),
        check_vma=False,
    )
```

```python
import math

import jax
import jax.numpy as jnp
from jax import lax
from jax.experimental import pallas as pl
from jax.experimental.pallas import tpu as pltpu
from jax.sharding import PartitionSpec as P

MASKED = -1e30
FIRST = ((3, 5),)
SECOND = (4, (6, 2), (1, 7))
LAST = (0,)
VMEM_BYTES = 24 * 1024 * 1024


def vmem_spec():
    return pl.BlockSpec(memory_space=pltpu.VMEM)


def smem_spec():
    return pl.BlockSpec(memory_space=pltpu.SMEM)


def hbm_spec():
    return pl.BlockSpec(memory_space=pltpu.HBM)


def in_hbm(array):
    return pltpu.with_memory_space_constraint(array, pltpu.HBM)


def params():
    return pltpu.CompilerParams(vmem_limit_bytes=VMEM_BYTES)


def spots_matrix(bits, steps):
    replicas, tokens = bits.shape
    shape = (replicas, 2 * steps, tokens)
    spread = jnp.broadcast_to(bits[:, None, :], shape)
    within = lax.broadcasted_iota(jnp.int32, shape, 1)
    token = lax.broadcasted_iota(jnp.int32, shape, 2)
    bit = jnp.where(within < steps, spread & 1, spread >> 1)
    hot = jnp.where((token % steps) == (within % steps), bit, 0)
    return hot.astype(jnp.float32).astype(jnp.bfloat16).reshape(replicas * 2 * steps, tokens)


def route_kernel(steps, *refs):
    sources, (wire_ref, bits_ref, moving_ref) = refs[:5], refs[5:8]
    locals_, sems = refs[8:13], refs[13]
    target_ref, slot_ref, *blocks = locals_
    copies = [
        pltpu.make_async_copy(source, local, sems.at[i])
        for i, (source, local) in enumerate(zip(sources, locals_))
    ]
    for copy in copies:
        copy.start()
    replicas, tokens = wire_ref.shape
    rows = tokens // steps
    shift = rows.bit_length()
    replica = lax.broadcasted_iota(jnp.int32, (replicas, rows), 0)
    order = lax.broadcasted_iota(jnp.int32, (replicas, rows), 1) << shift
    row = lax.broadcasted_iota(jnp.int32, (replicas, tokens), 1) // steps
    for copy in copies[:2]:
        copy.wait()
    mine = target_ref[...] == replica
    key = order + slot_ref[...]
    early = jnp.min(jnp.where(mine, key, (1 << 24) - 1), axis=1, keepdims=True)
    late = jnp.max(jnp.where(mine, key, -1), axis=1, keepdims=True)
    low = (1 << shift) - 1
    wire_ref[...] = jnp.where(row == (early & low), 1, 0) + jnp.where(row == (late & low), 2, 0)
    bits_ref[...] = jnp.where(row == (early >> shift), 1, 0) + jnp.where(row == (late >> shift), 2, 0)
    at = 0
    for copy, block in zip(copies[2:], blocks):
        copy.wait()
        features = block.shape[2]
        moving_ref[:, at : at + features] = block[...].reshape(tokens, features)
        at += features


def pack_kernel(steps, bits_ref, rows_ref, out_ref):
    hot = spots_matrix(bits_ref[...], steps)
    out_ref[...] = jnp.dot(hot, rows_ref[...], preferred_element_type=jnp.float32).astype(
        jnp.bfloat16
    )


def take_back(hot, rows):
    return lax.dot_general(
        hot, rows, (((0,), (0,)), ((), ())), preferred_element_type=jnp.float32
    ).astype(jnp.bfloat16)


def column_start(offset, groups, width):
    return pl.multiple_of(lax.rem(lax.axis_index("tp") + offset, groups) * width, width)


def flat(chunks):
    return [offset for chunk in chunks for offset in (chunk if isinstance(chunk, tuple) else [chunk])]


def give_out(chunks, products, outs):
    odd = (lax.axis_index("tp") & 1) == 1
    products, outs = iter(products), iter(outs)
    for chunk in chunks:
        if isinstance(chunk, tuple):
            one, other = next(products), next(products)
            next(outs)[...] = jnp.where(odd, one, other)
            next(outs)[...] = jnp.where(odd, other, one)
        else:
            next(outs)[...] = next(products)


def project(attended, columns):
    return jnp.dot(attended, columns, preferred_element_type=jnp.float32).astype(jnp.bfloat16)


def attend_kernel(
    steps,
    lengths_ref,
    bits_ref,
    got_ref,
    keys,
    values_hbm,
    weight_hbm,
    out_ref,
    outer_ref,
    inner_ref,
    values,
    weight,
    here,
    cache_scores,
    fresh_scores,
    cache_weights,
    fresh_weights,
    inverse,
    value_sem,
    weight_sems,
):
    value_copy = pltpu.make_async_copy(values_hbm, values, value_sem)
    value_copy.start()
    width = outer_ref.shape[1]
    groups = weight_hbm.shape[1] // width
    copies = [
        pltpu.make_async_copy(
            weight_hbm.at[:, pl.ds(column_start(offset, groups, width), width)],
            weight.at[i],
            weight_sems.at[i],
        )
        for i, offset in enumerate(flat(FIRST))
    ]
    for copy in copies:
        copy.start()
    rows, context, head_size = keys.shape
    features = out_ref.shape[1]
    heads = features // head_size
    pair = 2 * steps
    lines = heads * pair
    scale = 1.0 / math.sqrt(head_size) * math.log2(math.e)
    here[...] = take_back(spots_matrix(bits_ref[...], steps), got_ref[...])

    upper = lax.broadcasted_iota(jnp.int32, (lines, context), 0) % pair < steps
    column = lax.broadcasted_iota(jnp.int32, (lines, context), 1)
    fresh_line = lax.broadcasted_iota(jnp.int32, (lines, pair), 0) % pair
    fresh_column = lax.broadcasted_iota(jnp.int32, (lines, pair), 1)
    fresh_live = (fresh_line // steps == fresh_column // steps) & (fresh_column <= fresh_line)
    out_upper = lax.broadcasted_iota(jnp.int32, (lines, head_size), 0) % pair < steps

    def score(left, right):
        return lax.dot_general(
            left, right, (((1,), (1,)), ((), ())), preferred_element_type=jnp.float32
        )

    def mix(weights, block):
        return jnp.dot(weights, block, preferred_element_type=jnp.float32)

    for i in range(rows // 2):
        a, b = 2 * i, 2 * i + 1
        block = here[i * pair : (i + 1) * pair, :]
        queries = jnp.concatenate(
            [block[:, h * head_size : (h + 1) * head_size] for h in range(heads)], axis=0
        )
        limit = jnp.where(upper, lengths_ref[a], lengths_ref[b])
        scores = jnp.where(upper, score(queries, keys[a]), score(queries, keys[b]))
        cache_scores[i] = jnp.where(column < limit, scores * scale, MASKED)
        fresh = score(queries, block[:, features : features + head_size])
        fresh_scores[i] = jnp.where(fresh_live, fresh * scale, MASKED)

    for i in range(rows // 2):
        scores, fresh = cache_scores[i], fresh_scores[i]
        peak = jnp.maximum(
            jnp.max(scores, axis=1, keepdims=True), jnp.max(fresh, axis=1, keepdims=True)
        )
        weights = jnp.exp2(scores - peak).astype(jnp.bfloat16)
        weights_new = jnp.exp2(fresh - peak).astype(jnp.bfloat16)
        cache_weights[i] = weights
        fresh_weights[i] = weights_new
        total = jnp.sum(weights.astype(jnp.float32), axis=1, keepdims=True) + jnp.sum(
            weights_new.astype(jnp.float32), axis=1, keepdims=True
        )
        inverse[i] = jnp.broadcast_to(1.0 / total, (lines, head_size))

    value_copy.wait()
    for i in range(rows // 2):
        lot = slice(i * pair, (i + 1) * pair)
        weights = cache_weights[i]
        summed = jnp.where(out_upper, mix(weights, values[2 * i]), mix(weights, values[2 * i + 1]))
        summed = summed + mix(fresh_weights[i], here[lot, features + head_size :])
        result = (summed * inverse[i]).astype(jnp.bfloat16)
        for h in range(heads):
            out_ref[lot, h * head_size : (h + 1) * head_size] = result[h * pair : (h + 1) * pair]

    products = []
    for i, copy in enumerate(copies):
        copy.wait()
        products.append(project(out_ref[...], weight[i]))
    give_out(FIRST, products, (outer_ref, inner_ref))


def project_kernel(chunks, steps, attended_ref, weight_ref, *outs):
    width = outs[0].shape[1]
    groups = weight_ref.shape[1] // width
    products = [
        project(attended_ref[...], weight_ref[:, pl.ds(column_start(offset, groups, width), width)])
        for offset in flat(chunks)
    ]
    give_out(chunks, products, outs)


def wide(ref):
    return ref[...].astype(jnp.float32)


def relay_kernel(steps, *refs):
    total = wide(refs[0])
    for ref in refs[1:-1]:
        total = total + wide(ref)
    refs[-1][...] = total.astype(jnp.bfloat16)


def merge_kernel(steps, bits_ref, *refs):
    parts, out_ref = refs[:-1], refs[-1]
    total = wide(parts[0])
    for part in parts[1:]:
        total = total + wide(part)
    hot = spots_matrix(bits_ref[...], steps)
    out_ref[...] = jnp.dot(
        hot, total.astype(jnp.bfloat16), preferred_element_type=jnp.float32
    ).astype(jnp.bfloat16)


def unpack_kernel(steps, bits_ref, got_ref, out_ref):
    out_ref[...] = take_back(spots_matrix(bits_ref[...], steps), got_ref[...]).reshape(
        out_ref.shape
    )


def on_device(
    cache_keys,
    cache_values,
    cache_lengths,
    dest_replica,
    dest_slot,
    queries,
    new_keys,
    new_values,
    out_weight,
):
    replicas = lax.axis_size("rep")
    groups = lax.axis_size("tp")
    rows, _, context, head_size = cache_keys.shape
    steps, features = queries.shape[1:]
    tokens = rows * steps
    width = out_weight.shape[1] // groups
    spots = replicas * 2 * steps
    bf16 = jnp.bfloat16

    def out(shape, dtype=bf16):
        return jax.ShapeDtypeStruct(shape, dtype)

    def kernel(body, out_shape, in_specs, out_specs=None, scratch=(), cost=None):
        return pl.pallas_call(
            lambda *refs: body(steps, *refs),
            out_shape=out_shape,
            in_specs=in_specs,
            out_specs=vmem_spec() if out_specs is None else out_specs,
            scratch_shapes=scratch,
            compiler_params=params(),
            cost_estimate=cost,
        )

    full = features + 2 * head_size
    sources = (
        dest_replica.reshape(1, rows),
        dest_slot.reshape(1, rows),
        queries,
        new_keys,
        new_values,
    )
    wire, bits, moving = kernel(
        route_kernel,
        (
            out((replicas, tokens), jnp.int32),
            out((replicas, tokens), jnp.int32),
            out((tokens, full)),
        ),
        [hbm_spec()] * 5,
        (vmem_spec(),) * 3,
        [pltpu.VMEM(source.shape, source.dtype) for source in sources]
        + [pltpu.SemaphoreType.DMA((5,))],
    )(*(in_hbm(source) for source in sources))
    wire = lax.all_to_all(wire.reshape(replicas, 1, tokens), "rep", 0, 0, tiled=True)
    wire = wire.reshape(replicas, tokens)

    packed = kernel(pack_kernel, out((spots, full)), [vmem_spec()] * 2)(wire, moving)
    got = lax.all_to_all(packed.reshape(replicas, 2 * steps, full), "rep", 0, 0, tiled=True)

    lines = features // head_size * 2 * steps
    chunk = out((tokens, width))
    attended, outer, inner = kernel(
        attend_kernel,
        (out((tokens, features)), chunk, chunk),
        [smem_spec()] + [vmem_spec()] * 3 + [hbm_spec()] * 2,
        (vmem_spec(),) * 3,
        [
            pltpu.VMEM((rows, context, head_size), bf16),
            pltpu.VMEM((len(flat(FIRST)), features, width), bf16),
            pltpu.VMEM((tokens, full), bf16),
            pltpu.VMEM((rows // 2, lines, context), jnp.float32),
            pltpu.VMEM((rows // 2, lines, 2 * steps), jnp.float32),
            pltpu.VMEM((rows // 2, lines, context), bf16),
            pltpu.VMEM((rows // 2, lines, 2 * steps), bf16),
            pltpu.VMEM((rows // 2, lines, head_size), jnp.float32),
            pltpu.SemaphoreType.DMA(()),
            pltpu.SemaphoreType.DMA((len(flat(FIRST)),)),
        ],
    )(
        cache_lengths,
        bits,
        got.reshape(spots, full),
        cache_keys.reshape(rows, context, head_size),
        in_hbm(cache_values.reshape(rows, context, head_size)),
        in_hbm(out_weight),
    )

    def cross(block, by):
        return lax.ppermute(
            block, "tp", [(i, (i + (by if i % 2 else -by)) % groups) for i in range(groups)]
        )

    outer, inner = cross(outer, 1), cross(inner, -1)

    def projected(chunks):
        count = len(flat(chunks))
        return kernel(
            lambda steps, *refs: project_kernel(chunks, steps, *refs),
            (chunk,) * count,
            [vmem_spec()] * 2,
            (vmem_spec(),) * count,
            (),
            pl.CostEstimate(
                flops=2 * count * tokens * features * width,
                bytes_accessed=2 * count * features * width,
                transcendentals=0,
            ),
        )(attended, out_weight)

    far, first, second, *near = projected(SECOND)
    far = cross(far, 2)
    near = [cross(block, by) for block, by in zip(near, (1, -1))]
    (own,) = projected(LAST)

    def relay(*blocks):
        return kernel(relay_kernel, chunk, [vmem_spec()] * len(blocks))(*blocks)

    first = cross(relay(first, outer), -2)
    second = cross(relay(second, inner, far), 2)
    back = kernel(merge_kernel, out((spots, width)), [vmem_spec()] * 6)(
        bits, own, *near, first, second
    )
    back = lax.all_to_all(back.reshape(replicas, 2 * steps, width), "rep", 0, 0, tiled=True)
    return kernel(unpack_kernel, out((rows, steps, width)), [vmem_spec()] * 2)(
        wire, back.reshape(spots, width)
    )


def solution(mesh):
    return jax.shard_map(
        on_device,
        mesh=mesh,
        in_specs=(
            P("rep", "tp", None, None),
            P("rep", "tp", None, None),
            P("rep"),
            P("rep"),
            P("rep"),
            P("rep", None, "tp"),
            P("rep", None, "tp"),
            P("rep", None, "tp"),
            P("tp", None),
        ),
        out_specs=P("rep", None, "tp"),
        check_vma=False,
    )
```

```python
import math

import jax
import jax.numpy as jnp
from jax import lax
from jax.experimental import pallas as pl
from jax.experimental.pallas import tpu as pltpu
from jax.sharding import PartitionSpec as P

MASKED = -1e30
FIRST = ((3, 5),)
SECOND = (4, (6, 2))
THIRD = ((1, 7),)
LAST = (0,)
VMEM_BYTES = 24 * 1024 * 1024


def vmem_spec():
    return pl.BlockSpec(memory_space=pltpu.VMEM)


def smem_spec():
    return pl.BlockSpec(memory_space=pltpu.SMEM)


def hbm_spec():
    return pl.BlockSpec(memory_space=pltpu.HBM)


def in_hbm(array):
    return pltpu.with_memory_space_constraint(array, pltpu.HBM)


def params():
    return pltpu.CompilerParams(vmem_limit_bytes=VMEM_BYTES)


def spots_matrix(bits, steps):
    replicas, tokens = bits.shape
    shape = (replicas, 2 * steps, tokens)
    spread = jnp.broadcast_to(bits[:, None, :], shape)
    within = lax.broadcasted_iota(jnp.int32, shape, 1)
    token = lax.broadcasted_iota(jnp.int32, shape, 2)
    bit = jnp.where(within < steps, spread & 1, spread >> 1)
    hot = jnp.where((token % steps) == (within % steps), bit, 0)
    return hot.astype(jnp.float32).astype(jnp.bfloat16).reshape(replicas * 2 * steps, tokens)


def route_kernel(steps, *refs):
    sources, (wire_ref, bits_ref, moving_ref) = refs[:5], refs[5:8]
    locals_, sems = refs[8:13], refs[13]
    target_ref, slot_ref, *blocks = locals_
    copies = [
        pltpu.make_async_copy(source, local, sems.at[i])
        for i, (source, local) in enumerate(zip(sources, locals_))
    ]
    for copy in copies:
        copy.start()
    replicas, tokens = wire_ref.shape
    rows = tokens // steps
    shift = rows.bit_length()
    replica = lax.broadcasted_iota(jnp.int32, (replicas, rows), 0)
    order = lax.broadcasted_iota(jnp.int32, (replicas, rows), 1) << shift
    row = lax.broadcasted_iota(jnp.int32, (replicas, tokens), 1) // steps
    for copy in copies[:2]:
        copy.wait()
    mine = target_ref[...] == replica
    key = order + slot_ref[...]
    early = jnp.min(jnp.where(mine, key, (1 << 24) - 1), axis=1, keepdims=True)
    late = jnp.max(jnp.where(mine, key, -1), axis=1, keepdims=True)
    low = (1 << shift) - 1
    wire_ref[...] = jnp.where(row == (early & low), 1, 0) + jnp.where(row == (late & low), 2, 0)
    bits_ref[...] = jnp.where(row == (early >> shift), 1, 0) + jnp.where(row == (late >> shift), 2, 0)
    at = 0
    for copy, block in zip(copies[2:], blocks):
        copy.wait()
        features = block.shape[2]
        moving_ref[:, at : at + features] = block[...].reshape(tokens, features)
        at += features


def pack_kernel(steps, bits_ref, rows_ref, out_ref):
    hot = spots_matrix(bits_ref[...], steps)
    out_ref[...] = jnp.dot(hot, rows_ref[...], preferred_element_type=jnp.float32).astype(
        jnp.bfloat16
    )


def take_back(hot, rows):
    return lax.dot_general(
        hot, rows, (((0,), (0,)), ((), ())), preferred_element_type=jnp.float32
    ).astype(jnp.bfloat16)


def column_start(offset, groups, width):
    return pl.multiple_of(lax.rem(lax.axis_index("tp") + offset, groups) * width, width)


def flat(chunks):
    return [offset for chunk in chunks for offset in (chunk if isinstance(chunk, tuple) else [chunk])]


def give_out(chunks, products, outs):
    odd = (lax.axis_index("tp") & 1) == 1
    products, outs = iter(products), iter(outs)
    for chunk in chunks:
        if isinstance(chunk, tuple):
            one, other = next(products), next(products)
            next(outs)[...] = jnp.where(odd, one, other)
            next(outs)[...] = jnp.where(odd, other, one)
        else:
            next(outs)[...] = next(products)


def project(attended, columns):
    return jnp.dot(attended, columns, preferred_element_type=jnp.float32).astype(jnp.bfloat16)


def attend_kernel(
    steps,
    lengths_ref,
    bits_ref,
    got_ref,
    keys,
    values_hbm,
    weight_hbm,
    out_ref,
    outer_ref,
    inner_ref,
    values,
    weight,
    here,
    cache_scores,
    fresh_scores,
    cache_weights,
    fresh_weights,
    inverse,
    value_sem,
    weight_sems,
):
    value_copy = pltpu.make_async_copy(values_hbm, values, value_sem)
    value_copy.start()
    width = outer_ref.shape[1]
    groups = weight_hbm.shape[1] // width
    copies = [
        pltpu.make_async_copy(
            weight_hbm.at[:, pl.ds(column_start(offset, groups, width), width)],
            weight.at[i],
            weight_sems.at[i],
        )
        for i, offset in enumerate(flat(FIRST))
    ]
    for copy in copies:
        copy.start()
    rows, context, head_size = keys.shape
    features = out_ref.shape[1]
    heads = features // head_size
    pair = 2 * steps
    lines = heads * pair
    scale = 1.0 / math.sqrt(head_size) * math.log2(math.e)
    here[...] = take_back(spots_matrix(bits_ref[...], steps), got_ref[...])

    upper = lax.broadcasted_iota(jnp.int32, (lines, context), 0) % pair < steps
    column = lax.broadcasted_iota(jnp.int32, (lines, context), 1)
    fresh_line = lax.broadcasted_iota(jnp.int32, (lines, pair), 0) % pair
    fresh_column = lax.broadcasted_iota(jnp.int32, (lines, pair), 1)
    fresh_live = (fresh_line // steps == fresh_column // steps) & (fresh_column <= fresh_line)
    out_upper = lax.broadcasted_iota(jnp.int32, (lines, head_size), 0) % pair < steps

    def score(left, right):
        return lax.dot_general(
            left, right, (((1,), (1,)), ((), ())), preferred_element_type=jnp.float32
        )

    def mix(weights, block):
        return jnp.dot(weights, block, preferred_element_type=jnp.float32)

    for i in range(rows // 2):
        a, b = 2 * i, 2 * i + 1
        block = here[i * pair : (i + 1) * pair, :]
        queries = jnp.concatenate(
            [block[:, h * head_size : (h + 1) * head_size] for h in range(heads)], axis=0
        )
        limit = jnp.where(upper, lengths_ref[a], lengths_ref[b])
        scores = jnp.where(upper, score(queries, keys[a]), score(queries, keys[b]))
        cache_scores[i] = jnp.where(column < limit, scores * scale, MASKED)
        fresh = score(queries, block[:, features : features + head_size])
        fresh_scores[i] = jnp.where(fresh_live, fresh * scale, MASKED)

    for i in range(rows // 2):
        scores, fresh = cache_scores[i], fresh_scores[i]
        peak = jnp.maximum(
            jnp.max(scores, axis=1, keepdims=True), jnp.max(fresh, axis=1, keepdims=True)
        )
        weights = jnp.exp2(scores - peak).astype(jnp.bfloat16)
        weights_new = jnp.exp2(fresh - peak).astype(jnp.bfloat16)
        cache_weights[i] = weights
        fresh_weights[i] = weights_new
        total = jnp.sum(weights.astype(jnp.float32), axis=1, keepdims=True) + jnp.sum(
            weights_new.astype(jnp.float32), axis=1, keepdims=True
        )
        inverse[i] = jnp.broadcast_to(1.0 / total, (lines, head_size))

    value_copy.wait()
    for i in range(rows // 2):
        lot = slice(i * pair, (i + 1) * pair)
        weights = cache_weights[i]
        summed = jnp.where(out_upper, mix(weights, values[2 * i]), mix(weights, values[2 * i + 1]))
        summed = summed + mix(fresh_weights[i], here[lot, features + head_size :])
        result = (summed * inverse[i]).astype(jnp.bfloat16)
        for h in range(heads):
            out_ref[lot, h * head_size : (h + 1) * head_size] = result[h * pair : (h + 1) * pair]

    products = []
    for i, copy in enumerate(copies):
        copy.wait()
        products.append(project(out_ref[...], weight[i]))
    give_out(FIRST, products, (outer_ref, inner_ref))


def project_kernel(chunks, steps, attended_ref, weight_ref, *outs):
    width = outs[0].shape[1]
    groups = weight_ref.shape[1] // width
    products = [
        project(attended_ref[...], weight_ref[:, pl.ds(column_start(offset, groups, width), width)])
        for offset in flat(chunks)
    ]
    give_out(chunks, products, outs)


def last_kernel(steps, attended_ref, weight_ref, bits_ref, wire_ref, own_ref, spots_ref, places_ref):
    project_kernel(LAST, steps, attended_ref, weight_ref, own_ref)
    spots_ref[...] = spots_matrix(bits_ref[...], steps)
    places_ref[...] = spots_matrix(wire_ref[...], steps).astype(jnp.float32).T.astype(jnp.bfloat16)


def wide(ref):
    return ref[...].astype(jnp.float32)


def relay_kernel(steps, *refs):
    total = wide(refs[0])
    for ref in refs[1:-1]:
        total = total + wide(ref)
    refs[-1][...] = total.astype(jnp.bfloat16)


def merge_kernel(steps, spots_ref, *refs):
    parts, out_ref = refs[:-1], refs[-1]
    total = wide(parts[0])
    for part in parts[1:]:
        total = total + wide(part)
    out_ref[...] = jnp.dot(
        spots_ref[...], total.astype(jnp.bfloat16), preferred_element_type=jnp.float32
    ).astype(jnp.bfloat16)


def unpack_kernel(steps, places_ref, got_ref, out_ref):
    rows = jnp.dot(places_ref[...], got_ref[...], preferred_element_type=jnp.float32)
    out_ref[...] = rows.astype(jnp.bfloat16).reshape(out_ref.shape)


def on_device(
    cache_keys,
    cache_values,
    cache_lengths,
    dest_replica,
    dest_slot,
    queries,
    new_keys,
    new_values,
    out_weight,
):
    replicas = lax.axis_size("rep")
    groups = lax.axis_size("tp")
    rows, _, context, head_size = cache_keys.shape
    steps, features = queries.shape[1:]
    tokens = rows * steps
    width = out_weight.shape[1] // groups
    spots = replicas * 2 * steps
    bf16 = jnp.bfloat16

    def out(shape, dtype=bf16):
        return jax.ShapeDtypeStruct(shape, dtype)

    def kernel(body, out_shape, in_specs, out_specs=None, scratch=(), cost=None):
        return pl.pallas_call(
            lambda *refs: body(steps, *refs),
            out_shape=out_shape,
            in_specs=in_specs,
            out_specs=vmem_spec() if out_specs is None else out_specs,
            scratch_shapes=scratch,
            compiler_params=params(),
            cost_estimate=cost,
        )

    full = features + 2 * head_size
    sources = (
        dest_replica.reshape(1, rows),
        dest_slot.reshape(1, rows),
        queries,
        new_keys,
        new_values,
    )
    wire, bits, moving = kernel(
        route_kernel,
        (
            out((replicas, tokens), jnp.int32),
            out((replicas, tokens), jnp.int32),
            out((tokens, full)),
        ),
        [hbm_spec()] * 5,
        (vmem_spec(),) * 3,
        [pltpu.VMEM(source.shape, source.dtype) for source in sources]
        + [pltpu.SemaphoreType.DMA((5,))],
    )(*(in_hbm(source) for source in sources))
    wire = lax.all_to_all(wire.reshape(replicas, 1, tokens), "rep", 0, 0, tiled=True)
    wire = wire.reshape(replicas, tokens)

    packed = kernel(pack_kernel, out((spots, full)), [vmem_spec()] * 2)(wire, moving)
    got = lax.all_to_all(packed.reshape(replicas, 2 * steps, full), "rep", 0, 0, tiled=True)

    lines = features // head_size * 2 * steps
    chunk = out((tokens, width))
    attended, outer, inner = kernel(
        attend_kernel,
        (out((tokens, features)), chunk, chunk),
        [smem_spec()] + [vmem_spec()] * 3 + [hbm_spec()] * 2,
        (vmem_spec(),) * 3,
        [
            pltpu.VMEM((rows, context, head_size), bf16),
            pltpu.VMEM((len(flat(FIRST)), features, width), bf16),
            pltpu.VMEM((tokens, full), bf16),
            pltpu.VMEM((rows // 2, lines, context), jnp.float32),
            pltpu.VMEM((rows // 2, lines, 2 * steps), jnp.float32),
            pltpu.VMEM((rows // 2, lines, context), bf16),
            pltpu.VMEM((rows // 2, lines, 2 * steps), bf16),
            pltpu.VMEM((rows // 2, lines, head_size), jnp.float32),
            pltpu.SemaphoreType.DMA(()),
            pltpu.SemaphoreType.DMA((len(flat(FIRST)),)),
        ],
    )(
        cache_lengths,
        bits,
        got.reshape(spots, full),
        cache_keys.reshape(rows, context, head_size),
        in_hbm(cache_values.reshape(rows, context, head_size)),
        in_hbm(out_weight),
    )

    def cross(block, by):
        return lax.ppermute(
            block, "tp", [(i, (i + (by if i % 2 else -by)) % groups) for i in range(groups)]
        )

    outer, inner = cross(outer, 1), cross(inner, -1)

    def projected(chunks):
        count = len(flat(chunks))
        return kernel(
            lambda steps, *refs: project_kernel(chunks, steps, *refs),
            (chunk,) * count,
            [vmem_spec()] * 2,
            (vmem_spec(),) * count,
            (),
            pl.CostEstimate(
                flops=2 * count * tokens * features * width,
                bytes_accessed=2 * count * features * width,
                transcendentals=0,
            ),
        )(attended, out_weight)

    far, first, second = projected(SECOND)
    far = cross(far, 2)
    near = [cross(block, by) for block, by in zip(projected(THIRD), (1, -1))]
    own, spots_hot, places_hot = kernel(
        last_kernel,
        (chunk, out((spots, tokens)), out((tokens, spots))),
        [vmem_spec()] * 4,
        (vmem_spec(),) * 3,
    )(attended, out_weight, bits, wire)

    def relay(*blocks):
        return kernel(relay_kernel, chunk, [vmem_spec()] * len(blocks))(*blocks)

    first = cross(relay(first, outer), -2)
    second = cross(relay(second, inner, far), 2)
    back = kernel(merge_kernel, out((spots, width)), [vmem_spec()] * 6)(
        spots_hot, own, *near, first, second
    )
    back = lax.all_to_all(back.reshape(replicas, 2 * steps, width), "rep", 0, 0, tiled=True)
    return kernel(unpack_kernel, out((rows, steps, width)), [vmem_spec()] * 2)(
        places_hot, back.reshape(spots, width)
    )


def solution(mesh):
    return jax.shard_map(
        on_device,
        mesh=mesh,
        in_specs=(
            P("rep", "tp", None, None),
            P("rep", "tp", None, None),
            P("rep"),
            P("rep"),
            P("rep"),
            P("rep", None, "tp"),
            P("rep", None, "tp"),
            P("rep", None, "tp"),
            P("tp", None),
        ),
        out_specs=P("rep", None, "tp"),
        check_vma=False,
    )
```

```python
import math

import jax
import jax.numpy as jnp
from jax import lax
from jax.experimental import pallas as pl
from jax.experimental.pallas import tpu as pltpu
from jax.sharding import PartitionSpec as P

MASKED = -1e30
FIRST = ((3, 5),)
SECOND = (4, (6, 2))
THIRD = ((1, 7), 0)
VMEM_BYTES = 24 * 1024 * 1024


def vmem_spec():
    return pl.BlockSpec(memory_space=pltpu.VMEM)


def smem_spec():
    return pl.BlockSpec(memory_space=pltpu.SMEM)


def hbm_spec():
    return pl.BlockSpec(memory_space=pltpu.HBM)


def in_hbm(array):
    return pltpu.with_memory_space_constraint(array, pltpu.HBM)


def params():
    return pltpu.CompilerParams(vmem_limit_bytes=VMEM_BYTES)


def spots_matrix(bits, steps):
    replicas, tokens = bits.shape
    shape = (replicas, 2 * steps, tokens)
    spread = jnp.broadcast_to(bits[:, None, :], shape)
    within = lax.broadcasted_iota(jnp.int32, shape, 1)
    token = lax.broadcasted_iota(jnp.int32, shape, 2)
    bit = jnp.where(within < steps, spread & 1, spread >> 1)
    hot = jnp.where((token % steps) == (within % steps), bit, 0)
    return hot.astype(jnp.float32).astype(jnp.bfloat16).reshape(replicas * 2 * steps, tokens)


def route_kernel(steps, *refs):
    sources, (wire_ref, bits_ref, moving_ref) = refs[:5], refs[5:8]
    locals_, sems = refs[8:13], refs[13]
    target_ref, slot_ref, *blocks = locals_
    copies = [
        pltpu.make_async_copy(source, local, sems.at[i])
        for i, (source, local) in enumerate(zip(sources, locals_))
    ]
    for copy in copies:
        copy.start()
    replicas, tokens = wire_ref.shape
    rows = tokens // steps
    shift = rows.bit_length()
    replica = lax.broadcasted_iota(jnp.int32, (replicas, rows), 0)
    order = lax.broadcasted_iota(jnp.int32, (replicas, rows), 1) << shift
    row = lax.broadcasted_iota(jnp.int32, (replicas, tokens), 1) // steps
    for copy in copies[:2]:
        copy.wait()
    mine = target_ref[...] == replica
    key = order + slot_ref[...]
    early = jnp.min(jnp.where(mine, key, (1 << 24) - 1), axis=1, keepdims=True)
    late = jnp.max(jnp.where(mine, key, -1), axis=1, keepdims=True)
    low = (1 << shift) - 1
    wire_ref[...] = jnp.where(row == (early & low), 1, 0) + jnp.where(row == (late & low), 2, 0)
    bits_ref[...] = jnp.where(row == (early >> shift), 1, 0) + jnp.where(row == (late >> shift), 2, 0)
    at = 0
    for copy, block in zip(copies[2:], blocks):
        copy.wait()
        features = block.shape[2]
        moving_ref[:, at : at + features] = block[...].reshape(tokens, features)
        at += features


def pack_kernel(steps, bits_ref, rows_ref, out_ref):
    hot = spots_matrix(bits_ref[...], steps)
    out_ref[...] = jnp.dot(hot, rows_ref[...], preferred_element_type=jnp.float32).astype(
        jnp.bfloat16
    )


def take_back(hot, rows):
    return lax.dot_general(
        hot, rows, (((0,), (0,)), ((), ())), preferred_element_type=jnp.float32
    ).astype(jnp.bfloat16)


def column_start(offset, groups, width):
    return pl.multiple_of(lax.rem(lax.axis_index("tp") + offset, groups) * width, width)


def flat(chunks):
    return [offset for chunk in chunks for offset in (chunk if isinstance(chunk, tuple) else [chunk])]


def give_out(chunks, products, outs):
    odd = (lax.axis_index("tp") & 1) == 1
    products, outs = iter(products), iter(outs)
    for chunk in chunks:
        if isinstance(chunk, tuple):
            one, other = next(products), next(products)
            next(outs)[...] = jnp.where(odd, one, other)
            next(outs)[...] = jnp.where(odd, other, one)
        else:
            next(outs)[...] = next(products)


def project(attended, columns):
    return jnp.dot(attended, columns, preferred_element_type=jnp.float32).astype(jnp.bfloat16)


def attend_kernel(
    steps,
    lengths_ref,
    bits_ref,
    got_ref,
    keys,
    values_hbm,
    weight_hbm,
    out_ref,
    outer_ref,
    inner_ref,
    values,
    weight,
    here,
    cache_scores,
    fresh_scores,
    cache_weights,
    fresh_weights,
    inverse,
    value_sem,
    weight_sems,
):
    value_copy = pltpu.make_async_copy(values_hbm, values, value_sem)
    value_copy.start()
    width = outer_ref.shape[1]
    groups = weight_hbm.shape[1] // width
    copies = [
        pltpu.make_async_copy(
            weight_hbm.at[:, pl.ds(column_start(offset, groups, width), width)],
            weight.at[i],
            weight_sems.at[i],
        )
        for i, offset in enumerate(flat(FIRST))
    ]
    for copy in copies:
        copy.start()
    rows, context, head_size = keys.shape
    features = out_ref.shape[1]
    heads = features // head_size
    pair = 2 * steps
    lines = heads * pair
    scale = 1.0 / math.sqrt(head_size) * math.log2(math.e)
    here[...] = take_back(spots_matrix(bits_ref[...], steps), got_ref[...])

    upper = lax.broadcasted_iota(jnp.int32, (lines, context), 0) % pair < steps
    column = lax.broadcasted_iota(jnp.int32, (lines, context), 1)
    fresh_line = lax.broadcasted_iota(jnp.int32, (lines, pair), 0) % pair
    fresh_column = lax.broadcasted_iota(jnp.int32, (lines, pair), 1)
    fresh_live = (fresh_line // steps == fresh_column // steps) & (fresh_column <= fresh_line)
    out_upper = lax.broadcasted_iota(jnp.int32, (lines, head_size), 0) % pair < steps

    def score(left, right):
        return lax.dot_general(
            left, right, (((1,), (1,)), ((), ())), preferred_element_type=jnp.float32
        )

    def mix(weights, block):
        return jnp.dot(weights, block, preferred_element_type=jnp.float32)

    for i in range(rows // 2):
        a, b = 2 * i, 2 * i + 1
        block = here[i * pair : (i + 1) * pair, :]
        queries = jnp.concatenate(
            [block[:, h * head_size : (h + 1) * head_size] for h in range(heads)], axis=0
        )
        limit = jnp.where(upper, lengths_ref[a], lengths_ref[b])
        scores = jnp.where(upper, score(queries, keys[a]), score(queries, keys[b]))
        cache_scores[i] = jnp.where(column < limit, scores * scale, MASKED)
        fresh = score(queries, block[:, features : features + head_size])
        fresh_scores[i] = jnp.where(fresh_live, fresh * scale, MASKED)

    for i in range(rows // 2):
        scores, fresh = cache_scores[i], fresh_scores[i]
        peak = jnp.maximum(
            jnp.max(scores, axis=1, keepdims=True), jnp.max(fresh, axis=1, keepdims=True)
        )
        weights = jnp.exp2(scores - peak).astype(jnp.bfloat16)
        weights_new = jnp.exp2(fresh - peak).astype(jnp.bfloat16)
        cache_weights[i] = weights
        fresh_weights[i] = weights_new
        total = jnp.sum(weights.astype(jnp.float32), axis=1, keepdims=True) + jnp.sum(
            weights_new.astype(jnp.float32), axis=1, keepdims=True
        )
        inverse[i] = jnp.broadcast_to(1.0 / total, (lines, head_size))

    value_copy.wait()
    for i in range(rows // 2):
        lot = slice(i * pair, (i + 1) * pair)
        weights = cache_weights[i]
        summed = jnp.where(out_upper, mix(weights, values[2 * i]), mix(weights, values[2 * i + 1]))
        summed = summed + mix(fresh_weights[i], here[lot, features + head_size :])
        result = (summed * inverse[i]).astype(jnp.bfloat16)
        for h in range(heads):
            out_ref[lot, h * head_size : (h + 1) * head_size] = result[h * pair : (h + 1) * pair]

    products = []
    for i, copy in enumerate(copies):
        copy.wait()
        products.append(project(out_ref[...], weight[i]))
    give_out(FIRST, products, (outer_ref, inner_ref))


def project_kernel(chunks, steps, attended_ref, weight_ref, *outs):
    width = outs[0].shape[1]
    groups = weight_ref.shape[1] // width
    products = [
        project(attended_ref[...], weight_ref[:, pl.ds(column_start(offset, groups, width), width)])
        for offset in flat(chunks)
    ]
    give_out(chunks, products, outs)


def wide(ref):
    return ref[...].astype(jnp.float32)


def relay_kernel(steps, *refs):
    total = wide(refs[0])
    for ref in refs[1:-1]:
        total = total + wide(ref)
    refs[-1][...] = total.astype(jnp.bfloat16)


def merge_kernel(steps, bits_ref, *refs):
    parts, out_ref = refs[:-1], refs[-1]
    total = wide(parts[0])
    for part in parts[1:]:
        total = total + wide(part)
    hot = spots_matrix(bits_ref[...], steps)
    out_ref[...] = jnp.dot(
        hot, total.astype(jnp.bfloat16), preferred_element_type=jnp.float32
    ).astype(jnp.bfloat16)


def unpack_kernel(steps, bits_ref, got_ref, out_ref):
    out_ref[...] = take_back(spots_matrix(bits_ref[...], steps), got_ref[...]).reshape(
        out_ref.shape
    )


def on_device(
    cache_keys,
    cache_values,
    cache_lengths,
    dest_replica,
    dest_slot,
    queries,
    new_keys,
    new_values,
    out_weight,
):
    replicas = lax.axis_size("rep")
    groups = lax.axis_size("tp")
    rows, _, context, head_size = cache_keys.shape
    steps, features = queries.shape[1:]
    tokens = rows * steps
    width = out_weight.shape[1] // groups
    spots = replicas * 2 * steps
    bf16 = jnp.bfloat16

    def out(shape, dtype=bf16):
        return jax.ShapeDtypeStruct(shape, dtype)

    def kernel(body, out_shape, in_specs, out_specs=None, scratch=(), cost=None):
        return pl.pallas_call(
            lambda *refs: body(steps, *refs),
            out_shape=out_shape,
            in_specs=in_specs,
            out_specs=vmem_spec() if out_specs is None else out_specs,
            scratch_shapes=scratch,
            compiler_params=params(),
            cost_estimate=cost,
        )

    full = features + 2 * head_size
    sources = (
        dest_replica.reshape(1, rows),
        dest_slot.reshape(1, rows),
        queries,
        new_keys,
        new_values,
    )
    wire, bits, moving = kernel(
        route_kernel,
        (
            out((replicas, tokens), jnp.int32),
            out((replicas, tokens), jnp.int32),
            out((tokens, full)),
        ),
        [hbm_spec()] * 5,
        (vmem_spec(),) * 3,
        [pltpu.VMEM(source.shape, source.dtype) for source in sources]
        + [pltpu.SemaphoreType.DMA((5,))],
    )(*(in_hbm(source) for source in sources))
    wire = lax.all_to_all(wire.reshape(replicas, 1, tokens), "rep", 0, 0, tiled=True)
    wire = wire.reshape(replicas, tokens)

    packed = kernel(pack_kernel, out((spots, full)), [vmem_spec()] * 2)(wire, moving)
    got = lax.all_to_all(packed.reshape(replicas, 2 * steps, full), "rep", 0, 0, tiled=True)

    lines = features // head_size * 2 * steps
    chunk = out((tokens, width))
    attended, outer, inner = kernel(
        attend_kernel,
        (out((tokens, features)), chunk, chunk),
        [smem_spec()] + [vmem_spec()] * 3 + [hbm_spec()] * 2,
        (vmem_spec(),) * 3,
        [
            pltpu.VMEM((rows, context, head_size), bf16),
            pltpu.VMEM((len(flat(FIRST)), features, width), bf16),
            pltpu.VMEM((tokens, full), bf16),
            pltpu.VMEM((rows // 2, lines, context), jnp.float32),
            pltpu.VMEM((rows // 2, lines, 2 * steps), jnp.float32),
            pltpu.VMEM((rows // 2, lines, context), bf16),
            pltpu.VMEM((rows // 2, lines, 2 * steps), bf16),
            pltpu.VMEM((rows // 2, lines, head_size), jnp.float32),
            pltpu.SemaphoreType.DMA(()),
            pltpu.SemaphoreType.DMA((len(flat(FIRST)),)),
        ],
    )(
        cache_lengths,
        bits,
        got.reshape(spots, full),
        cache_keys.reshape(rows, context, head_size),
        in_hbm(cache_values.reshape(rows, context, head_size)),
        in_hbm(out_weight),
    )

    def cross(block, by):
        return lax.ppermute(
            block, "tp", [(i, (i + (by if i % 2 else -by)) % groups) for i in range(groups)]
        )

    outer, inner = cross(outer, 1), cross(inner, -1)

    def projected(chunks):
        count = len(flat(chunks))
        return kernel(
            lambda steps, *refs: project_kernel(chunks, steps, *refs),
            (chunk,) * count,
            [vmem_spec()] * 2,
            (vmem_spec(),) * count,
            (),
            pl.CostEstimate(
                flops=2 * count * tokens * features * width,
                bytes_accessed=2 * count * features * width,
                transcendentals=0,
            ),
        )(attended, out_weight)

    far, first, second = projected(SECOND)
    far = cross(far, 2)
    *near, own = projected(THIRD)
    near = [cross(block, by) for block, by in zip(near, (1, -1))]

    def relay(*blocks):
        return kernel(relay_kernel, chunk, [vmem_spec()] * len(blocks))(*blocks)

    first = cross(relay(first, outer), -2)
    second = cross(relay(second, inner, far), 2)
    back = kernel(merge_kernel, out((spots, width)), [vmem_spec()] * 6)(
        bits, own, *near, first, second
    )
    back = lax.all_to_all(back.reshape(replicas, 2 * steps, width), "rep", 0, 0, tiled=True)
    return kernel(unpack_kernel, out((rows, steps, width)), [vmem_spec()] * 2)(
        wire, back.reshape(spots, width)
    )


def solution(mesh):
    return jax.shard_map(
        on_device,
        mesh=mesh,
        in_specs=(
            P("rep", "tp", None, None),
            P("rep", "tp", None, None),
            P("rep"),
            P("rep"),
            P("rep"),
            P("rep", None, "tp"),
            P("rep", None, "tp"),
            P("rep", None, "tp"),
            P("tp", None),
        ),
        out_specs=P("rep", None, "tp"),
        check_vma=False,
    )
```
